128 devices in a mesh: dp: 8 (over y, core), ep: 16 (over x, z).
Axes of the slice: x: 4, y: 4, z: 4, core: 2. Of those that a mesh axis runs over, the one named last changes fastest.
Arguments:
- tokens: bfloat16 [2048, 2880], P(('dp', 'ep')), may hold values from -40 to 40
- norm_gain: float32 [2880], replicated, may hold values from 0.1 to 1.9
- expert_ids: int32 [2048, 4], P(('dp', 'ep')), may hold values from 0 to 63, all different within a row; in each aligned block of 16 rows (0 to 15, 16 to 31, ...) at most 2 rows name the same one
- gate_weights: float32 [2048, 4], P(('dp', 'ep')), may hold values from 0.1 to 1
- expert_gate_up: bfloat16 [128, 2, 2880, 720], P(('dp', 'ep')), may hold values from -0.109375 to 0.109375
- expert_down: bfloat16 [128, 720, 2880], P(('dp', 'ep')), may hold values from -0.15625 to 0.15625
- queries: bfloat16 [512, 2, 2048], P(('dp', 'ep')), may hold values from -8 to 8
- new_cache: bfloat16 [512, 2, 2, 256], P(('dp', 'ep')), may hold values from -8 to 8
- cache_pool: bfloat16 [16384, 2, 64, 256], P(('dp', 'ep')), may hold values from -30 to 30
- page_table: int32 [512, 32], P(('dp', 'ep')), may hold values from 0 to 127, as said below
- cache_length: int32 [512], P(('dp', 'ep')), may hold values from 1 to 2048, as said below
- sink_logits: float32 [32], replicated, may hold values from 2 to 8
Outputs:
- expert_mixed: bfloat16 [2048, 2880], P(('dp', 'ep'))
- attention_out: bfloat16 [512, 2, 2048], P(('dp', 'ep'))
The draws below stay inside these ranges and needn't reach their ends.
Inputs may be any that keep to these rules, and one draw needn't show every extreme that they name: `expert_ids`: each row names 4 different experts; among the 16 rows of one device no expert is named more than 2 times. `page_table`: the rows of the 4 requests of one device together hold each of 0 to 127 once. `cache_length`: in every draw the 4 requests of some device all have length 2048.
All inputs are finite; a program needn't handle non-finite values.
Results may differ from the reference program's by a relative error of at most 0.008.
Values may be sent and summed in bfloat16 or wider, within the bound.
A program may use at most 128 MiB of HBM per device.

```python
import math
import jax
import jax.numpy as jnp
import numpy as np
from jax import lax

D = 2880
QH = 32
KVH = 4
HD = 64
H_EXP = 1440
TOP = 4
PAGE = 64
MAXLEN = 2048
MOE_DEV = 16
ATT_DEV = 4
EXPERTS = 64
CAP = 2
TOKENS = 2048
ATT_REQ = 512
MAXP = 32
PAGES_DEV = 128
POOL = 16384
N_DP = 8
N_EP = 16


def log_scale(key, shape, lower, upper):
    return jnp.exp(jax.random.uniform(key, shape, jnp.float32, math.log(lower), math.log(upper)))


def draw_tokens(key, part):
    key = jax.random.fold_in(key, 3)
    subkeys = jax.random.split(key, 3)
    row_scale = log_scale(subkeys[0], (TOKENS, 1), 0.3, 3.0)
    col_scale = log_scale(subkeys[1], (1, D), 0.3, 3.0)
    raw_values = jnp.clip(jax.random.normal(subkeys[2], (TOKENS, D), jnp.float32), -3.0, 3.0)
    return (raw_values * row_scale * col_scale).astype(jnp.bfloat16)


def draw_queries(key, part):
    key = jax.random.fold_in(key, 5)
    result = jnp.clip(jax.random.normal(key, (ATT_REQ, 2, QH, HD), jnp.float32), -4.0, 4.0)
    return result.reshape(ATT_REQ, 2, QH * HD).astype(jnp.bfloat16)


def draw_new_cache(key, part):
    key = jax.random.fold_in(key, 7)
    result = jnp.clip(jax.random.normal(key, (ATT_REQ, 2, 2, KVH, HD), jnp.float32), -4.0, 4.0)
    return result.reshape(ATT_REQ, 2, 2, KVH * HD).astype(jnp.bfloat16)


def draw_cache_pool(key, part):
    key = jax.random.fold_in(key, 9)
    subkeys = jax.random.split(key, 3)
    row_scale = log_scale(subkeys[0], (POOL, 2, PAGE, 1), 0.3, 3.0)
    col_scale = log_scale(subkeys[1], (1, 2, 1, KVH * HD), 0.3, 3.0)
    raw_values = jnp.clip(jax.random.normal(subkeys[2], (POOL, 2, PAGE, KVH * HD), jnp.float32), -3.0, 3.0)
    return (raw_values * row_scale * col_scale).astype(jnp.bfloat16)


def draw_page_table(key, part):
    key = jax.random.fold_in(key, 11)
    blocks = ATT_REQ // ATT_DEV
    orders = jax.vmap(lambda one_key: jax.random.permutation(one_key, PAGES_DEV))(jax.random.split(key, blocks))
    return orders.reshape(ATT_REQ, MAXP).astype(jnp.int32)


def draw_cache_length(key, part):
    key = jax.random.fold_in(key, 13)
    subkeys = jax.random.split(key, 2)
    levels = jax.random.randint(subkeys[0], (ATT_REQ,), 0, 64)
    lengths = 1 + levels * levels * levels * (MAXLEN - 1) // (63 * 63 * 63)
    full_block = jax.random.randint(subkeys[1], (), 0, ATT_REQ // ATT_DEV)
    owners = jnp.arange(ATT_REQ, dtype=jnp.int32) // ATT_DEV
    return jnp.where(owners == full_block, MAXLEN, lengths).astype(jnp.int32)


def steps_of(own_key, shape, pieces, smallest, largest):
    gain, own = 1.0, jax.random.fold_in(own_key, 6)
    for dim, shards_of in pieces:
        steps = jnp.exp(jax.random.uniform(jax.random.fold_in(own, dim), (shards_of,), jnp.float32, smallest / len(pieces), largest / len(pieces)))
        gain = gain * jnp.repeat(steps, shape[dim] // shards_of).reshape([-1 if axis == dim else 1 for axis in range(len(shape))])
    return gain


def routed_block(key, own, number, rows, amount, top, limit, slope):
    order = jax.random.permutation(key, amount)
    packed, ordinary = shares(amount, rows * top, limit, slope, True), shares(amount, rows * top, limit, slope, False)
    places = jnp.arange(amount)

    def named(sizes, rotation):
        used = int((sizes > 0).sum())
        fixed = max(1, used // 4)
        shifted = fixed + (places - fixed + rotation * (used - fixed)) % max(1, amount - fixed)
        return jnp.zeros((amount,), jnp.int32).at[order[jnp.where(places < fixed, places, shifted)]].set(jnp.asarray(sizes, jnp.int32))

    sizes = jnp.where(number % 4 == 0, named(packed, number // 4), named(ordinary, number - number // 4 - 1))
    mixed = jax.random.permutation(jax.random.fold_in(own, 3), amount)
    source_of, receiver = mixed[0:amount // 2 * 2:2], mixed[1:amount // 2 * 2:2]
    margin = jnp.minimum(sizes[source_of] - 1, limit - sizes[receiver]) // 2
    margin = jnp.where((source_of == order[0]) | (receiver == order[0]) | (sizes[receiver] == 0), 0, jnp.maximum(margin, 0))
    shifted = jax.random.randint(jax.random.fold_in(own, 4), (amount // 2,), 0, 1 << 20) % (margin + 1)
    sizes = sizes.at[source_of].add(-shifted).at[receiver].add(shifted)
    members = jnp.searchsorted(jnp.cumsum(sizes), jnp.arange(rows * top), side="right").astype(jnp.int32)
    grid = members.reshape(top, rows).T
    grid = grid[jax.random.permutation(jax.random.fold_in(own, 1), rows)]
    rotation = jax.random.randint(jax.random.fold_in(own, 2), (rows, 1), 0, top)
    return jnp.take_along_axis(grid, (jnp.arange(top)[None, :] + rotation) % top, axis=1)


def shares(amount, total, most, slope, full):
    loads = [(1 << 20) // math.isqrt(standing ** slope) + 1 for standing in range(1, amount + 1)]
    largest = most if full else min(most, max(-(-total // amount), total * loads[0] // sum(loads)))
    least = 1 if total - largest >= amount - 1 else 0
    counts, spare = [largest] + [least] * (amount - 1), total - largest - least * (amount - 1)
    while spare > 0:
        free = [i for i in range(1, amount) if counts[i] < largest] or [i for i in range(1, amount) if counts[i] < most]
        whole, budget = sum([loads[i] for i in free]), spare
        for i in free:
            more = min(most - counts[i], max(1, budget * loads[i] // whole), spare)
            counts[i] = counts[i] + more
            spare = spare - more
    return np.array(counts)


def centred(stream_key, dims, spread, most, cuts=(), held_as=jnp.bfloat16):
    factor_of = steps_of(stream_key, dims, cuts, -0.22, 0.18) if cuts else 1.0
    drawn = jax.random.normal(stream_key, dims, jnp.float32) * spread * factor_of
    return jnp.minimum(jnp.maximum(drawn, -most), most).astype(held_as)


def setup_inputs(seed: int = 0) -> dict:
    key_of = jax.random.split(jax.random.key(seed), 13)
    tokens = draw_tokens(jax.random.fold_in(key_of[12], 71), 0)
    norm_gain = jnp.clip(1.0 + 0.18 * jax.random.normal(key_of[1], (D,), jnp.float32), 0.1, 1.9)
    expert_ids_keys = jax.random.split(jax.random.fold_in(key_of[2], 1), TOKENS // MOE_DEV)
    expert_ids_turns = jax.random.permutation(jax.random.fold_in(key_of[2], 3), TOKENS // MOE_DEV)
    expert_ids = jax.vmap(lambda own, number: routed_block(jax.random.fold_in(key_of[2], 2), own, number, MOE_DEV, EXPERTS, TOP, CAP, 2))(expert_ids_keys, expert_ids_turns).reshape((TOKENS, TOP))
    gate_weights = jnp.clip(0.1 + 0.9 * jax.random.uniform(key_of[3], (TOKENS, TOP), jnp.float32) ** steps_of(key_of[3], (TOKENS, TOP), ((0, 128),), -0.2, 0.2), 0.1, 1.0)
    expert_gate_up = centred(key_of[4], (2 * EXPERTS, 2, D, H_EXP // 2), D ** -0.5, 0.109375, ((0, 128),))
    expert_down = centred(key_of[5], (2 * EXPERTS, H_EXP // 2, D), H_EXP ** -0.5, 0.15625, ((0, 128),))
    queries = draw_queries(jax.random.fold_in(key_of[12], 71), 0)
    new_cache = draw_new_cache(jax.random.fold_in(key_of[12], 71), 0)
    cache_pool = draw_cache_pool(jax.random.fold_in(key_of[12], 71), 0)
    page_table = draw_page_table(jax.random.fold_in(key_of[12], 71), 0)
    cache_length = draw_cache_length(jax.random.fold_in(key_of[12], 71), 0)
    sink_logits = jnp.clip(jax.random.uniform(key_of[11], (QH,), jnp.float32, 2.0, 8.0), 2.0, 8.0)
    return {"tokens": tokens, "norm_gain": norm_gain, "expert_ids": expert_ids, "gate_weights": gate_weights, "expert_gate_up": expert_gate_up, "expert_down": expert_down, "queries": queries, "new_cache": new_cache, "cache_pool": cache_pool, "page_table": page_table, "cache_length": cache_length, "sink_logits": sink_logits}


EPS = 1e-05

def expert_apply(row_block, gate_up, down_rows):
    gate_value = jnp.dot(row_block, gate_up[0], preferred_element_type=jnp.float32)
    up_value = jnp.dot(row_block, gate_up[1], preferred_element_type=jnp.float32)
    hidden = ((up_value + 1.0) * gate_value * jax.nn.sigmoid(1.702 * gate_value)).astype(jnp.bfloat16)
    return jnp.dot(hidden, down_rows, preferred_element_type=jnp.float32)

def normalize(tokens, norm_gain):
    wide_tokens = tokens.astype(jnp.float32)
    mean_square = lax.optimization_barrier(jnp.mean(wide_tokens * wide_tokens, axis=1, keepdims=True))
    return (wide_tokens * lax.rsqrt(mean_square + EPS) * norm_gain).astype(jnp.bfloat16)

def attend(queries, new_cache, cache_pool, page_table, cache_length, sink_logits):
    requests = queries.shape[0]
    groups = QH // KVH
    scale_factor = 1.0 / math.sqrt(HD)
    gathered = cache_pool[page_table]
    cached_keys = gathered[:, :, 0].reshape(requests, MAXLEN, KVH, HD).astype(jnp.float32)
    cached_values = gathered[:, :, 1].reshape(requests, MAXLEN, KVH, HD).astype(jnp.float32)
    query_heads = queries.reshape(requests, 2, KVH, groups, HD).astype(jnp.float32)
    new_keys = new_cache[:, :, 0].reshape(requests, 2, KVH, HD).astype(jnp.float32)
    new_values = new_cache[:, :, 1].reshape(requests, 2, KVH, HD).astype(jnp.float32)
    cache_scores = jnp.einsum('ajkgd,alkd->ajkgl', query_heads, cached_keys) * scale_factor
    fresh_scores = jnp.einsum('ajkgd,aikd->ajkgi', query_heads, new_keys) * scale_factor
    positions = jnp.arange(MAXLEN, dtype=jnp.int32)
    cache_mask = (positions[None, :] < cache_length[:, None])[:, None, None, None, :]
    fresh_mask = (jnp.arange(2)[None, :] <= jnp.arange(2)[:, None])[None, :, None, None, :]
    scores = jnp.concatenate([cache_scores, fresh_scores], axis=-1)
    keep_mask = jnp.concatenate([jnp.broadcast_to(cache_mask, cache_scores.shape), jnp.broadcast_to(fresh_mask, fresh_scores.shape)], axis=-1)
    masked = jnp.where(keep_mask, scores, -1e+30)
    sink_grid = sink_logits.reshape(KVH, groups)[None, None]
    ceiling = jnp.maximum(lax.optimization_barrier(jnp.max(masked, axis=-1)), sink_grid)
    exp_terms = jnp.where(keep_mask, jnp.exp(masked - ceiling[..., None]), 0.0)
    denominator = jnp.exp(sink_grid - ceiling) + lax.optimization_barrier(jnp.sum(exp_terms, axis=-1))
    weights = (exp_terms / denominator[..., None]).astype(jnp.bfloat16)
    all_values = jnp.concatenate([cached_values, new_values], axis=1)
    result = jnp.einsum('ajkgl,alkd->ajkgd', weights.astype(jnp.float32), all_values)
    return result.astype(jnp.bfloat16).reshape(requests, 2, QH * HD)

def reference(tokens, norm_gain, expert_ids, gate_weights, expert_gate_up, expert_down, queries, new_cache, cache_pool, page_table, cache_length, sink_logits):
    devices = N_DP * N_EP
    normed = normalize(tokens, norm_gain)
    flat_ids = expert_ids.reshape(devices, MOE_DEV * TOP)
    one_hot = (flat_ids[:, :, None] == jnp.arange(EXPERTS, dtype=jnp.int32)[None, None, :]).astype(jnp.int32)
    earlier = jnp.cumsum(one_hot, axis=1) - one_hot
    slot_index = lax.optimization_barrier(jnp.sum(earlier * one_hot, axis=2)).astype(jnp.int32)
    column = jnp.arange(devices, dtype=jnp.int32)[:, None] * CAP + slot_index
    pick_number = jnp.arange(TOKENS * TOP, dtype=jnp.int32).reshape(devices, MOE_DEV * TOP)
    slot_table = jnp.full((EXPERTS, devices * CAP), TOKENS * TOP, jnp.int32).at[flat_ids, column].set(pick_number)
    padded_rows = jnp.concatenate([normed, jnp.zeros((1, D), jnp.bfloat16)], axis=0)
    padded_gates = jnp.concatenate([gate_weights.reshape(-1), jnp.zeros((1,), jnp.float32)])
    gate_up_whole = expert_gate_up.reshape(EXPERTS, 2, 2, D, H_EXP // 2)
    down_whole = expert_down.reshape(EXPERTS, H_EXP, D)

    def one_expert(accumulated, expert):
        halves = gate_up_whole[expert]
        gate_up = jnp.concatenate([halves[0], halves[1]], axis=-1)
        picks_here = slot_table[expert]
        token_here = picks_here // TOP
        outputs = expert_apply(padded_rows[token_here], gate_up, down_whole[expert])
        scaled = outputs * padded_gates[picks_here][:, None]
        return (accumulated.at[token_here].add(scaled), expert)
    accumulated = lax.scan(one_expert, jnp.zeros((TOKENS + 1, D), jnp.float32), jnp.arange(EXPERTS, dtype=jnp.int32))[0]
    expert_mixed = (tokens.astype(jnp.float32) + accumulated[:TOKENS]).astype(jnp.bfloat16)

    def attend_block(grouped):
        return attend(grouped[0], grouped[1], grouped[2], grouped[3], grouped[4], sink_logits)
    grouped = (queries.reshape(devices, ATT_DEV, 2, QH * HD), new_cache.reshape(devices, ATT_DEV, 2, 2, KVH * HD), cache_pool.reshape(devices, PAGES_DEV, 2, PAGE, KVH * HD), page_table.reshape(devices, ATT_DEV, MAXP), cache_length.reshape(devices, ATT_DEV))
    attention_out = lax.map(attend_block, grouped).reshape(ATT_REQ, 2, QH * HD)
    return (expert_mixed, attention_out)
```

```python
import functools

import jax
import jax.numpy as jnp
from jax import lax
from jax.experimental import pallas as pl
from jax.experimental.pallas import tpu as pltpu
from jax.sharding import PartitionSpec as P

D = 2880
H = 720
WIDE = 3072
QUADS = 6
PEERS = 64
ROWS = 96
GROUP = 16
BATCH = 32
EPS = 1e-05
NEG = -1e30
F32 = jnp.float32
BF16 = jnp.bfloat16
MESH = pl.DeviceIdType.MESH
NT = (((1,), (1,)), ((), ()))


def dot(a, b):
    return jnp.dot(a, b, preferred_element_type=F32)


def dot_nt(a, b):
    return lax.dot_general(a, b, NT, preferred_element_type=F32)


def iota(shape, axis):
    return lax.broadcasted_iota(jnp.int32, shape, axis)


def kernel(
    tokens, gain, ids, gates, gate_up, down, queries, fresh, pool, table, length, sinks,
    mixed, attended,
    own, sib, away, landed, back, home, x_rows, o_rows, weight_hi, weight_lo, total, partial, partial_in,
    gu_v, down_v, pool_v, spread, scores, outs,
    load_sem, pair_send, pair_recv, send_sem, recv_sem, back_send, home_recv,
):
    dp = lax.axis_index("dp")
    ep = lax.axis_index("ep")
    x, z = ep // 4, ep % 4
    y, c = dp // 2, dp % 2
    step = 37 - 10 * c

    def peer(i, sign):
        o = (step * i) % PEERS
        px = (x + 4 + sign * (o // 16)) % 4
        py = (y + 4 + sign * ((o // 4) % 4)) % 4
        pz = (z + 4 + sign * (o % 4)) % 4
        return (py * 2 + c, px * 4 + pz)

    sibling = (y * 2 + 1 - c, ep)

    pool_copy = pltpu.make_async_copy(pool, pool_v, load_sem.at[0])
    gu_copy = pltpu.make_async_copy(gate_up.at[0], gu_v, load_sem.at[1])
    down_copy = pltpu.make_async_copy(down.at[0], down_v, load_sem.at[2])
    pool_copy.start()
    gu_copy.start()
    down_copy.start()

    barrier = pltpu.get_barrier_semaphore()
    pl.semaphore_signal(barrier, inc=1, device_id=sibling, device_id_type=MESH)

    def greet(i, carry):
        pl.semaphore_signal(barrier, inc=1, device_id=peer(i, 1), device_id_type=MESH)
        return carry

    lax.fori_loop(1, PEERS, greet, 0)

    wide = tokens[...].astype(F32)
    mean_square = jnp.sum(wide * wide, axis=1, keepdims=True) * (1.0 / D)
    own[:, 0:D] = (wide * lax.rsqrt(mean_square + EPS) * gain[...]).astype(BF16)
    lane = iota((16, 128), 1)
    named = jnp.zeros((16, 128), F32)
    gate_hi = jnp.zeros((16, 128), F32)
    gate_lo = jnp.zeros((16, 128), F32)
    for k in range(4):
        id_k = ids[:, k : k + 1]
        gate_k = gates[:, k : k + 1]
        hi_k = gate_k.astype(BF16).astype(F32)
        named = jnp.where(id_k == lane, 1.0, named)
        gate_hi = jnp.where(id_k + 64 == lane, hi_k, gate_hi)
        gate_lo = jnp.where(id_k + 64 == lane, gate_k - hi_k, gate_lo)
    earlier = (iota((16, 16), 1) < iota((16, 16), 0)).astype(BF16)
    rank = dot(earlier, named.astype(BF16))
    code = named * (1.0 + rank)
    tail = own[:, 2816:2944].astype(F32)
    own[:, 2816:2944] = jnp.where(lane < 64, tail, gate_lo).astype(BF16)
    own[:, 2944:3072] = jnp.where(lane < 64, code, gate_hi).astype(BF16)

    pl.semaphore_wait(barrier, PEERS)
    pair = pltpu.make_async_remote_copy(
        src_ref=own, dst_ref=sib, send_sem=pair_send.at[0], recv_sem=pair_recv.at[0],
        device_id=sibling, device_id_type=MESH,
    )
    pair.start()
    o_rows[:, 2816:3072] = jnp.zeros((4 * BATCH, 256), BF16)
    pair.wait_recv()

    def chunk(n):
        return jnp.concatenate([own[:, n * 128 : n * 128 + 128], sib[:, n * 128 : n * 128 + 128]], axis=0)

    stacked = jnp.concatenate(
        [jnp.concatenate([chunk(4 * q + b) for b in range(4)], axis=0) for q in range(QUADS)], axis=1
    )
    codes22 = jnp.concatenate([chunk(22)] * 4, axis=0)
    codes23 = jnp.concatenate([chunk(23)] * 4, axis=0)

    def expert_at(i):
        o = (step * i) & 63
        px = (x + (o >> 4)) & 3
        py = (y + ((o >> 2) & 3)) & 3
        pz = (z + (o & 3)) & 3
        return (py * 2 + c) * 8 + ((px * 4 + pz) >> 1)

    def send(i, carry):
        pltpu.make_async_remote_copy(
            src_ref=away.at[i], dst_ref=landed.at[i], send_sem=send_sem.at[i], recv_sem=recv_sem.at[i],
            device_id=peer(i, 1), device_id_type=MESH,
        ).start()
        return carry

    for k in range(PEERS // GROUP):
        row = iota((256, 128), 0)
        col = iota((256, 128), 1)
        expert = expert_at(GROUP * k + (row >> 4))
        pick = (expert == col).astype(BF16)
        found = dot_nt(pick, codes23)
        slot = row & 3
        chosen = (
            (((row >> 2) & 3) == (col >> 5))
            & (((col >> 4) & 1) == (slot >> 1))
            & (found == ((slot & 1) + 1).astype(F32))
        )
        packed = dot(chosen.astype(BF16), stacked).astype(BF16)
        for q in range(QUADS):
            away[GROUP * k : GROUP * (k + 1), 16 * q : 16 * q + 16, :] = packed[
                :, 128 * q : 128 * q + 128
            ].reshape(GROUP, 16, 128)
        lax.fori_loop(max(GROUP * k, 1), GROUP * (k + 1), send, 0)
    own_copy = pltpu.make_async_copy(away.at[0], landed.at[0], load_sem.at[3])
    own_copy.start()

    for k in range(PEERS // GROUP):
        row = iota((128, 256), 0)
        col = iota((128, 256), 1)
        wide_row = iota((256, 128), 0)
        wide_col = iota((256, 128), 1)
        expert = expert_at(GROUP * k + (wide_row >> 4))
        pick = (expert == wide_col).astype(BF16)
        pick_gate = (expert + 64 == wide_col).astype(BF16)
        found = dot_nt(codes23, pick)
        slot = col & 3
        chosen = (
            (((col >> 2) & 3) == (row >> 5))
            & (((row >> 4) & 1) == (slot >> 1))
            & (found == ((slot & 1) + 1).astype(F32))
        )
        weight_hi[:, 256 * k : 256 * k + 256] = jnp.where(chosen, dot_nt(codes23, pick_gate), 0.0).astype(BF16)
        weight_lo[:, 256 * k : 256 * k + 256] = jnp.where(chosen, dot_nt(codes22, pick_gate), 0.0).astype(BF16)

    def fold(g):
        return (((iota((512, 256), 0) & 63) + 64 * g) == iota((512, 256), 1)).astype(BF16)

    own_head = (iota((64, 512), 1) >> 6) == (iota((64, 512), 0) & 7)
    for g in range(4):
        part = queries[:, 512 * g : 512 * g + 512].astype(F32) * 0.125
        part = jnp.broadcast_to(part[:, None, :], (8, 8, 512)).reshape(64, 512)
        part = jnp.where(own_head, part, 0.0).astype(BF16)
        folded = dot(part, fold(g)).astype(BF16)
        spread[:, 16 * g : 16 * g + 16, :] = folded.reshape(4, 16, 256)
    take = iota((16, 16), 1)
    take_at = iota((16, 16), 0)
    fresh_keys = dot(((2 * take_at == take) & (take_at < 8)).astype(BF16), fresh[...]).astype(BF16)
    fresh_values = dot(((2 * take_at + 1 == take) & (take_at < 8)).astype(BF16), fresh[...]).astype(BF16)
    sink_row = iota((64, 32), 0)
    sink_at = (sink_row >> 4) * 8 + (sink_row & 7) == iota((64, 32), 1)
    sink = jnp.sum(jnp.where(sink_at, sinks[...], 0.0), axis=1, keepdims=True)
    pool_copy.wait()

    def request(r, carry):
        query = spread[r]
        limit = length[r]
        fresh_col = iota((64, 16), 1)
        fresh_row = iota((64, 16), 0)
        fresh_ok = ((fresh_col >> 1) == r) & ((fresh_col & 1) <= ((fresh_row >> 3) & 1))
        fresh_scores = jnp.where(fresh_ok, dot_nt(query, fresh_keys), NEG)
        top = jnp.maximum(jnp.max(fresh_scores, axis=1, keepdims=True), sink)
        best = jnp.full((64, 256), NEG, F32)
        for b in range(8):
            keys = jnp.concatenate([pool_v[table[r, 4 * b + i], 0] for i in range(4)], axis=0)
            block = dot_nt(query, keys)
            block = jnp.where(iota((64, 256), 1) + 256 * b < limit, block, NEG)
            scores[:, 256 * b : 256 * b + 256] = block
            best = jnp.maximum(best, block)
        top = jnp.maximum(top, jnp.max(best, axis=1, keepdims=True))
        fresh_exp = jnp.where(fresh_ok, jnp.exp(fresh_scores - top), 0.0)
        result = dot(fresh_exp.astype(BF16), fresh_values)
        summed = jnp.zeros((64, 256), F32)
        for b in range(8):
            ok = iota((64, 256), 1) + 256 * b < limit
            block = jnp.where(ok, jnp.exp(scores[:, 256 * b : 256 * b + 256] - top), 0.0)
            summed = summed + block
            values = jnp.concatenate([pool_v[table[r, 4 * b + i], 1] for i in range(4)], axis=0)
            result = result + dot(block.astype(BF16), values)
        denominator = (
            jnp.exp(sink - top)
            + jnp.sum(fresh_exp, axis=1, keepdims=True)
            + jnp.sum(summed, axis=1, keepdims=True)
        )
        outs[r] = (result / denominator).astype(BF16)
        return carry

    lax.fori_loop(0, 4, request, 0)
    for g in range(4):
        part = outs[:, 16 * g : 16 * g + 16, :].reshape(64, 256)
        part = jnp.where(own_head, dot_nt(part, fold(g)), 0.0)
        attended[:, 512 * g : 512 * g + 512] = jnp.sum(part.reshape(8, 8, 512), axis=1).astype(BF16)

    own_copy.wait()
    gu_copy.wait()
    down_copy.wait()

    def arrive(i, carry):
        pltpu.make_async_remote_copy(
            src_ref=away.at[i], dst_ref=landed.at[i], send_sem=send_sem.at[i], recv_sem=recv_sem.at[i],
            device_id=sibling, device_id_type=MESH,
        ).wait_recv()
        return carry

    def give(i, carry):
        pltpu.make_async_remote_copy(
            src_ref=back.at[i], dst_ref=home.at[i], send_sem=back_send.at[i], recv_sem=home_recv.at[i],
            device_id=peer(i, -1), device_id_type=MESH,
        ).start()
        return carry

    to_row = iota((256, 256), 0)
    to_col = iota((256, 256), 1)
    unpack = (
        ((to_row >> 6) == ((to_col >> 2) & 3))
        & (((to_row >> 2) & 15) == (to_col >> 4))
        & ((to_row & 3) == (to_col & 3))
    ).astype(BF16)
    repack = (
        ((to_col >> 6) == ((to_row >> 2) & 3))
        & (((to_col >> 2) & 15) == (to_row >> 4))
        & ((to_row & 3) == (to_col & 3))
    ).astype(BF16)

    def batch(n, carry):
        start = n * BATCH
        lax.fori_loop(jnp.maximum(start, 1), start + BATCH, arrive, 0)
        for s in range(BATCH // GROUP):
            at = start + s * GROUP
            block = jnp.concatenate(
                [landed[pl.ds(at, GROUP), 16 * q : 16 * q + 16, :].reshape(256, 128) for q in range(QUADS)], axis=1
            )
            flat = dot(unpack, block).astype(BF16)
            for q in range(QUADS):
                for b in range(4):
                    x_rows[64 * s : 64 * s + 64, (4 * q + b) * 128 : (4 * q + b) * 128 + 128] = flat[
                        64 * b : 64 * b + 64, 128 * q : 128 * q + 128
                    ]
        rows = x_rows[:, 0:D]
        gate_value = dot(rows, gu_v[0])
        up_value = dot(rows, gu_v[1])
        hidden = ((up_value + 1.0) * gate_value * jax.nn.sigmoid(1.702 * gate_value)).astype(BF16)
        o_rows[:, 0:D] = dot(hidden, down_v[...]).astype(BF16)
        for s in range(BATCH // GROUP):
            at = start + s * GROUP
            block = jnp.concatenate(
                [
                    jnp.concatenate(
                        [
                            o_rows[64 * s : 64 * s + 64, (4 * q + b) * 128 : (4 * q + b) * 128 + 128]
                            for b in range(4)
                        ],
                        axis=0,
                    )
                    for q in range(QUADS)
                ],
                axis=1,
            )
            flat = dot(repack, block).astype(BF16)
            for q in range(QUADS):
                back[pl.ds(at, GROUP), 16 * q : 16 * q + 16, :] = flat[:, 128 * q : 128 * q + 128].reshape(
                    GROUP, 16, 128
                )
        lax.fori_loop(jnp.maximum(start, 1), start + BATCH, give, 0)
        return carry

    lax.fori_loop(0, PEERS // BATCH, batch, 0)
    own_back = pltpu.make_async_copy(back.at[0], home.at[0], load_sem.at[4])
    own_back.start()

    def returned(i, carry):
        pltpu.make_async_remote_copy(
            src_ref=back.at[i], dst_ref=home.at[i], send_sem=back_send.at[i], recv_sem=home_recv.at[i],
            device_id=sibling, device_id_type=MESH,
        ).wait_recv()
        return carry

    own_back.wait()
    for k in range(PEERS // GROUP):
        lax.fori_loop(max(GROUP * k, 1), GROUP * (k + 1), returned, 0)
        block = jnp.concatenate(
            [home[GROUP * k : GROUP * (k + 1), 16 * q : 16 * q + 16, :].reshape(256, 128) for q in range(QUADS)],
            axis=1,
        )
        here = dot(weight_hi[:, 256 * k : 256 * k + 256], block) + dot(weight_lo[:, 256 * k : 256 * k + 256], block)
        if k == 0:
            total[...] = here
        else:
            total[...] += here
    for q in range(QUADS):
        for b in range(4):
            partial[:, (4 * q + b) * 128 : (4 * q + b) * 128 + 128] = total[
                32 * b + 16 : 32 * b + 32, 128 * q : 128 * q + 128
            ]
    swap = pltpu.make_async_remote_copy(
        src_ref=partial, dst_ref=partial_in, send_sem=pair_send.at[1], recv_sem=pair_recv.at[1],
        device_id=sibling, device_id_type=MESH,
    )
    swap.start()

    def sent(i, carry):
        pltpu.make_async_remote_copy(
            src_ref=away.at[i], dst_ref=landed.at[i], send_sem=send_sem.at[i], recv_sem=recv_sem.at[i],
            device_id=sibling, device_id_type=MESH,
        ).wait_send()
        pltpu.make_async_remote_copy(
            src_ref=back.at[i], dst_ref=home.at[i], send_sem=back_send.at[i], recv_sem=home_recv.at[i],
            device_id=sibling, device_id_type=MESH,
        ).wait_send()
        return carry

    lax.fori_loop(1, PEERS, sent, 0)
    pair.wait_send()
    swap.wait()
    for n in range(23):
        q, b = n // 4, n % 4
        width = min(128, D - 128 * n)
        at = slice(128 * n, 128 * n + width)
        mine = total[32 * b : 32 * b + 16, 128 * q : 128 * q + width]
        mixed[:, at] = (tokens[:, at].astype(F32) + mine + partial_in[:, at]).astype(BF16)


def local(
    tokens, norm_gain, expert_ids, gate_weights, expert_gate_up, expert_down,
    queries, new_cache, cache_pool, page_table, cache_length, sink_logits,
):
    vmem = pl.BlockSpec(memory_space=pltpu.VMEM)
    smem = pl.BlockSpec(memory_space=pltpu.SMEM)
    hbm = pl.BlockSpec(memory_space=pl.ANY)
    dma = pltpu.SemaphoreType.DMA
    packed = pltpu.VMEM((PEERS, ROWS, 128), BF16)
    mixed, attended = pl.pallas_call(
        kernel,
        out_shape=(
            jax.ShapeDtypeStruct((16, D), BF16),
            jax.ShapeDtypeStruct((8, 2048), BF16),
        ),
        in_specs=[vmem, vmem, vmem, vmem, hbm, hbm, vmem, vmem, hbm, smem, smem, vmem],
        out_specs=(vmem, vmem),
        scratch_shapes=[
            pltpu.VMEM((16, WIDE), BF16),
            pltpu.VMEM((16, WIDE), BF16),
            packed,
            packed,
            packed,
            packed,
            pltpu.VMEM((4 * BATCH, WIDE), BF16),
            pltpu.VMEM((4 * BATCH, WIDE), BF16),
            pltpu.VMEM((128, 1024), BF16),
            pltpu.VMEM((128, 1024), BF16),
            pltpu.VMEM((128, 768), F32),
            pltpu.VMEM((16, WIDE), F32),
            pltpu.VMEM((16, WIDE), F32),
            pltpu.VMEM((2, D, H), BF16),
            pltpu.VMEM((H, D), BF16),
            pltpu.VMEM((128, 2, 64, 256), BF16),
            pltpu.VMEM((4, 64, 256), BF16),
            pltpu.VMEM((64, 2048), F32),
            pltpu.VMEM((4, 64, 256), BF16),
            dma((5,)),
            dma((2,)),
            dma((2,)),
            dma((PEERS,)),
            dma((PEERS,)),
            dma((PEERS,)),
            dma((PEERS,)),
        ],
        compiler_params=pltpu.CompilerParams(
            collective_id=0, has_side_effects=True, vmem_limit_bytes=56 * 2**20
        ),
        name="decode",
    )(
        tokens, norm_gain.reshape(1, D), expert_ids, gate_weights, expert_gate_up, expert_down,
        queries.reshape(8, 2048), new_cache.reshape(16, 256), cache_pool, page_table, cache_length,
        sink_logits.reshape(1, 32),
    )
    return mixed, attended.reshape(queries.shape)


def solution(mesh):
    rows = P(("dp", "ep"))
    placed = (rows, P(), rows, rows, rows, rows, rows, rows, rows, rows, rows, P())
    return jax.shard_map(
        local, mesh=mesh, in_specs=placed, out_specs=(rows, rows), check_vma=False
    )
```

```python
import functools

import jax
import jax.numpy as jnp
from jax import lax
from jax.experimental import pallas as pl
from jax.experimental.pallas import tpu as pltpu
from jax.sharding import PartitionSpec as P

D = 2880
H = 720
WIDE = 3072
QUADS = 6
PEERS = 64
ROWS = 96
GROUP = 16
BATCH = GROUP
EPS = 1e-05
NEG = -1e30
F32 = jnp.float32
BF16 = jnp.bfloat16
MESH = pl.DeviceIdType.MESH
NT = (((1,), (1,)), ((), ()))


def dot(a, b):
    return jnp.dot(a, b, preferred_element_type=F32)


def dot_nt(a, b):
    return lax.dot_general(a, b, NT, preferred_element_type=F32)


def iota(shape, axis):
    return lax.broadcasted_iota(jnp.int32, shape, axis)


def kernel(
    tokens_in, gain_in, ids_in, gates_in, gate_up, down, queries_in, fresh_in, pool, table_in, length_in, sinks_in,
    mixed_out, attended_out,
    tokens, gain, ids, gates, queries, fresh, sinks, table, length, mixed, attended,
    own, sib, away, landed, back, home, x_rows, o_rows, weight_hi, weight_lo, total, partial, partial_in,
    gu_v, down_v, pool_v, spread, scores, outs,
    load_sem, pair_send, pair_recv, send_sem, recv_sem, home_recv,
):
    dp = lax.axis_index("dp")
    ep = lax.axis_index("ep")
    x, z = ep // 4, ep % 4
    y, c = dp // 2, dp % 2
    step = 37 - 10 * c

    def peer(i, sign):
        o = (step * i) % PEERS
        px = (x + 4 + sign * (o // 16)) % 4
        py = (y + 4 + sign * ((o // 4) % 4)) % 4
        pz = (z + 4 + sign * (o % 4)) % 4
        return (py * 2 + c, px * 4 + pz)

    sibling = (y * 2 + 1 - c, ep)

    first = [(tokens_in, tokens), (ids_in, ids), (gates_in, gates), (gain_in, gain)]
    later = [(queries_in, queries), (fresh_in, fresh), (sinks_in, sinks), (table_in, table), (length_in, length)]
    first = [pltpu.make_async_copy(a, b, load_sem.at[3 + n]) for n, (a, b) in enumerate(first)]
    later = [pltpu.make_async_copy(a, b, load_sem.at[7 + n]) for n, (a, b) in enumerate(later)]
    for copy in first:
        copy.start()
    pool_copy = pltpu.make_async_copy(pool, pool_v, load_sem.at[0])
    gu_copy = pltpu.make_async_copy(gate_up.at[0], gu_v, load_sem.at[1])
    down_copy = pltpu.make_async_copy(down.at[0], down_v, load_sem.at[2])
    pool_copy.start()
    gu_copy.start()
    down_copy.start()
    for copy in later:
        copy.start()

    barrier = pltpu.get_barrier_semaphore()
    pl.semaphore_signal(barrier, inc=1, device_id=sibling, device_id_type=MESH)

    def greet(i, carry):
        pl.semaphore_signal(barrier, inc=1, device_id=peer(i, 1), device_id_type=MESH)
        return carry

    lax.fori_loop(1, PEERS, greet, 0)

    for copy in first:
        copy.wait()
    wide = tokens[...].astype(F32)
    mean_square = jnp.sum(wide * wide, axis=1, keepdims=True) * (1.0 / D)
    own[:, 0:D] = (wide * lax.rsqrt(mean_square + EPS) * gain[...].reshape(1, D)).astype(BF16)
    lane = iota((16, 128), 1)
    id_cols = ids[...].T
    gate_cols = gates[...].T
    named = jnp.zeros((16, 128), F32)
    gate_hi = jnp.zeros((16, 128), F32)
    gate_lo = jnp.zeros((16, 128), F32)
    for k in range(4):
        id_k = id_cols[:, k : k + 1]
        gate_k = gate_cols[:, k : k + 1]
        hi_k = gate_k.astype(BF16).astype(F32)
        named = jnp.where(id_k == lane, 1.0, named)
        gate_hi = jnp.where(id_k + 64 == lane, hi_k, gate_hi)
        gate_lo = jnp.where(id_k + 64 == lane, gate_k - hi_k, gate_lo)
    earlier = (iota((16, 16), 1) < iota((16, 16), 0)).astype(BF16)
    rank = dot(earlier, named.astype(BF16))
    code = named * (1.0 + rank)
    tail = own[:, 2816:2944].astype(F32)
    own[:, 2816:2944] = jnp.where(lane < 64, tail, gate_lo).astype(BF16)
    own[:, 2944:3072] = jnp.where(lane < 64, code, gate_hi).astype(BF16)

    pl.semaphore_wait(barrier, PEERS)
    pair = pltpu.make_async_remote_copy(
        src_ref=own, dst_ref=sib, send_sem=pair_send.at[0], recv_sem=pair_recv.at[0],
        device_id=sibling, device_id_type=MESH,
    )
    pair.start()
    o_rows[:, 2816:3072] = jnp.zeros((4 * BATCH, 256), BF16)
    pair.wait_recv()

    def chunk(n):
        return jnp.concatenate([own[:, n * 128 : n * 128 + 128], sib[:, n * 128 : n * 128 + 128]], axis=0)

    stacked = jnp.concatenate(
        [jnp.concatenate([chunk(4 * q + b) for b in range(4)], axis=0) for q in range(QUADS)], axis=1
    )
    codes22 = jnp.concatenate([chunk(22)] * 4, axis=0)
    codes23 = jnp.concatenate([chunk(23)] * 4, axis=0)

    def expert_at(i):
        o = (step * i) & 63
        px = (x + (o >> 4)) & 3
        py = (y + ((o >> 2) & 3)) & 3
        pz = (z + (o & 3)) & 3
        return (py * 2 + c) * 8 + ((px * 4 + pz) >> 1)

    def send(i, carry):
        pltpu.make_async_remote_copy(
            src_ref=away.at[i], dst_ref=landed.at[i], send_sem=send_sem.at[0], recv_sem=recv_sem.at[i // GROUP],
            device_id=peer(i, 1), device_id_type=MESH,
        ).start()
        return carry

    for k in range(PEERS // GROUP):
        row = iota((256, 128), 0)
        col = iota((256, 128), 1)
        expert = expert_at(GROUP * k + (row >> 4))
        pick = (expert == col).astype(BF16)
        found = dot_nt(pick, codes23)
        slot = row & 3
        chosen = (
            (((row >> 2) & 3) == (col >> 5))
            & (((col >> 4) & 1) == (slot >> 1))
            & (found == ((slot & 1) + 1).astype(F32))
        )
        packed = dot(chosen.astype(BF16), stacked).astype(BF16)
        for q in range(QUADS):
            away[GROUP * k : GROUP * (k + 1), 16 * q : 16 * q + 16, :] = packed[
                :, 128 * q : 128 * q + 128
            ].reshape(GROUP, 16, 128)
        lax.fori_loop(max(GROUP * k, 1), GROUP * (k + 1), send, 0)
    own_copy = pltpu.make_async_copy(away.at[0], landed.at[0], recv_sem.at[0])
    own_copy.start()

    for k in range(PEERS // GROUP):
        row = iota((128, 256), 0)
        col = iota((128, 256), 1)
        wide_row = iota((256, 128), 0)
        wide_col = iota((256, 128), 1)
        expert = expert_at(GROUP * k + (wide_row >> 4))
        pick = (expert == wide_col).astype(BF16)
        pick_gate = (expert + 64 == wide_col).astype(BF16)
        found = dot_nt(codes23, pick)
        slot = col & 3
        chosen = (
            (((col >> 2) & 3) == (row >> 5))
            & (((row >> 4) & 1) == (slot >> 1))
            & (found == ((slot & 1) + 1).astype(F32))
        )
        weight_hi[:, 256 * k : 256 * k + 256] = jnp.where(chosen, dot_nt(codes23, pick_gate), 0.0).astype(BF16)
        weight_lo[:, 256 * k : 256 * k + 256] = jnp.where(chosen, dot_nt(codes22, pick_gate), 0.0).astype(BF16)

    for copy in later:
        copy.wait()
    def fold(g):
        return (((iota((512, 256), 0) & 63) + 64 * g) == iota((512, 256), 1)).astype(BF16)

    own_head = (iota((64, 512), 1) >> 6) == (iota((64, 512), 0) & 7)
    for g in range(4):
        part = jnp.concatenate([queries[r, :, 512 * g : 512 * g + 512].astype(F32) for r in range(4)], axis=0) * 0.125
        part = jnp.broadcast_to(part[:, None, :], (8, 8, 512)).reshape(64, 512)
        part = jnp.where(own_head, part, 0.0).astype(BF16)
        folded = dot(part, fold(g)).astype(BF16)
        spread[:, 16 * g : 16 * g + 16, :] = folded.reshape(4, 16, 256)
    take = iota((16, 16), 1)
    take_at = iota((16, 16), 0)
    fresh_rows = jnp.concatenate([fresh[r, i].astype(F32) for r in range(4) for i in range(2)], axis=0).astype(BF16)
    fresh_keys = dot(((2 * take_at == take) & (take_at < 8)).astype(BF16), fresh_rows).astype(BF16)
    fresh_values = dot(((2 * take_at + 1 == take) & (take_at < 8)).astype(BF16), fresh_rows).astype(BF16)
    sink_row = iota((64, 32), 0)
    sink_at = (sink_row >> 4) * 8 + (sink_row & 7) == iota((64, 32), 1)
    sink = jnp.sum(jnp.where(sink_at, sinks[...], 0.0), axis=1, keepdims=True)
    pool_copy.wait()

    def request(r, carry):
        query = spread[r]
        limit = length[r]
        fresh_col = iota((64, 16), 1)
        fresh_row = iota((64, 16), 0)
        fresh_ok = ((fresh_col >> 1) == r) & ((fresh_col & 1) <= ((fresh_row >> 3) & 1))
        fresh_scores = jnp.where(fresh_ok, dot_nt(query, fresh_keys), NEG)
        top = jnp.maximum(jnp.max(fresh_scores, axis=1, keepdims=True), sink)
        best = jnp.full((64, 256), NEG, F32)
        for b in range(8):
            keys = jnp.concatenate([pool_v[table[r, 4 * b + i], 0] for i in range(4)], axis=0)
            block = dot_nt(query, keys)
            block = jnp.where(iota((64, 256), 1) + 256 * b < limit, block, NEG)
            scores[:, 256 * b : 256 * b + 256] = block
            best = jnp.maximum(best, block)
        top = jnp.maximum(top, jnp.max(best, axis=1, keepdims=True))
        fresh_exp = jnp.where(fresh_ok, jnp.exp(fresh_scores - top), 0.0)
        result = dot(fresh_exp.astype(BF16), fresh_values)
        summed = jnp.zeros((64, 256), F32)
        for b in range(8):
            ok = iota((64, 256), 1) + 256 * b < limit
            block = jnp.where(ok, jnp.exp(scores[:, 256 * b : 256 * b + 256] - top), 0.0)
            summed = summed + block
            values = jnp.concatenate([pool_v[table[r, 4 * b + i], 1] for i in range(4)], axis=0)
            result = result + dot(block.astype(BF16), values)
        denominator = (
            jnp.exp(sink - top)
            + jnp.sum(fresh_exp, axis=1, keepdims=True)
            + jnp.sum(summed, axis=1, keepdims=True)
        )
        outs[r] = (result / denominator).astype(BF16)
        return carry

    lax.fori_loop(0, 4, request, 0)
    for g in range(4):
        part = outs[:, 16 * g : 16 * g + 16, :].reshape(64, 256)
        part = jnp.where(own_head, dot_nt(part, fold(g)), 0.0)
        part = jnp.sum(part.reshape(8, 8, 512), axis=1)
        for r in range(4):
            attended[r, :, 512 * g : 512 * g + 512] = part[2 * r : 2 * r + 2].astype(BF16)

    attended_copy = pltpu.make_async_copy(attended, attended_out, load_sem.at[12])
    attended_copy.start()

    gu_copy.wait()
    down_copy.wait()

    def outward(at, sem):
        return pltpu.make_async_remote_copy(
            src_ref=away.at[at], dst_ref=landed.at[at], send_sem=send_sem.at[0], recv_sem=recv_sem.at[sem],
            device_id=sibling, device_id_type=MESH,
        )

    def homeward(at, sem):
        return pltpu.make_async_remote_copy(
            src_ref=back.at[at], dst_ref=home.at[at], send_sem=send_sem.at[1], recv_sem=home_recv.at[sem],
            device_id=sibling, device_id_type=MESH,
        )

    def give(i, carry):
        pltpu.make_async_remote_copy(
            src_ref=back.at[i], dst_ref=home.at[i], send_sem=send_sem.at[1], recv_sem=home_recv.at[i // GROUP],
            device_id=peer(i, -1), device_id_type=MESH,
        ).start()
        return carry

    to_row = iota((256, 256), 0)
    to_col = iota((256, 256), 1)
    unpack = (
        ((to_row >> 6) == ((to_col >> 2) & 3))
        & (((to_row >> 2) & 15) == (to_col >> 4))
        & ((to_row & 3) == (to_col & 3))
    ).astype(BF16)
    repack = (
        ((to_col >> 6) == ((to_row >> 2) & 3))
        & (((to_col >> 2) & 15) == (to_row >> 4))
        & ((to_row & 3) == (to_col & 3))
    ).astype(BF16)

    def batch(n, carry):
        start = n * BATCH
        outward(pl.ds(start, GROUP), n).wait_recv()
        for s in range(BATCH // GROUP):
            at = start + s * GROUP
            block = jnp.concatenate(
                [landed[pl.ds(at, GROUP), 16 * q : 16 * q + 16, :].reshape(256, 128) for q in range(QUADS)], axis=1
            )
            flat = dot(unpack, block).astype(BF16)
            for q in range(QUADS):
                for b in range(4):
                    x_rows[64 * s : 64 * s + 64, (4 * q + b) * 128 : (4 * q + b) * 128 + 128] = flat[
                        64 * b : 64 * b + 64, 128 * q : 128 * q + 128
                    ]
        rows = x_rows[:, 0:D]
        gate_value = dot_nt(rows, gu_v[0])
        up_value = dot_nt(rows, gu_v[1])
        hidden = ((up_value + 1.0) * gate_value * jax.nn.sigmoid(1.702 * gate_value)).astype(BF16)
        o_rows[:, 0:D] = dot(hidden, down_v[...]).astype(BF16)
        for s in range(BATCH // GROUP):
            at = start + s * GROUP
            block = jnp.concatenate(
                [
                    jnp.concatenate(
                        [
                            o_rows[64 * s : 64 * s + 64, (4 * q + b) * 128 : (4 * q + b) * 128 + 128]
                            for b in range(4)
                        ],
                        axis=0,
                    )
                    for q in range(QUADS)
                ],
                axis=1,
            )
            flat = dot(repack, block).astype(BF16)
            for q in range(QUADS):
                back[pl.ds(at, GROUP), 16 * q : 16 * q + 16, :] = flat[:, 128 * q : 128 * q + 128].reshape(
                    GROUP, 16, 128
                )
        lax.fori_loop(jnp.maximum(start, 1), start + BATCH, give, 0)
        return carry

    lax.fori_loop(0, PEERS // BATCH, batch, 0)
    own_back = pltpu.make_async_copy(back.at[0], home.at[0], home_recv.at[0])
    own_back.start()
    for k in range(PEERS // GROUP):
        homeward(pl.ds(GROUP * k, GROUP), k).wait_recv()
        block = jnp.concatenate(
            [home[GROUP * k : GROUP * (k + 1), 16 * q : 16 * q + 16, :].reshape(256, 128) for q in range(QUADS)],
            axis=1,
        )
        here = dot(weight_hi[:, 256 * k : 256 * k + 256], block) + dot(weight_lo[:, 256 * k : 256 * k + 256], block)
        if k == 0:
            total[...] = here
        else:
            total[...] += here
    for q in range(QUADS):
        for b in range(4):
            partial[:, (4 * q + b) * 128 : (4 * q + b) * 128 + 128] = total[
                32 * b + 16 : 32 * b + 32, 128 * q : 128 * q + 128
            ]
    swap = pltpu.make_async_remote_copy(
        src_ref=partial, dst_ref=partial_in, send_sem=pair_send.at[1], recv_sem=pair_recv.at[1],
        device_id=sibling, device_id_type=MESH,
    )
    swap.start()

    outward(pl.ds(1, PEERS - 1), 0).wait_send()
    homeward(pl.ds(1, PEERS - 1), 0).wait_send()
    pair.wait_send()
    swap.wait()
    for n in range(23):
        q, b = n // 4, n % 4
        width = min(128, D - 128 * n)
        at = slice(128 * n, 128 * n + width)
        mine = total[32 * b : 32 * b + 16, 128 * q : 128 * q + width]
        mixed[:, at] = (tokens[:, at].astype(F32) + mine + partial_in[:, at]).astype(BF16)
    mixed_copy = pltpu.make_async_copy(mixed, mixed_out, load_sem.at[13])
    mixed_copy.start()
    attended_copy.wait()
    mixed_copy.wait()


def finish(mixed_in, attended_in, mixed, attended):
    mixed[...] = mixed_in[...]
    attended[...] = attended_in[...]


def local(
    tokens, norm_gain, expert_ids, gate_weights, expert_gate_up, expert_down,
    queries, new_cache, cache_pool, page_table, cache_length, sink_logits,
):
    hbm = pl.BlockSpec(memory_space=pl.ANY)
    vmem = pl.BlockSpec(memory_space=pltpu.VMEM)
    dma = pltpu.SemaphoreType.DMA
    packed = pltpu.VMEM((PEERS, ROWS, 128), BF16)
    shapes = (
        jax.ShapeDtypeStruct((16, D), BF16),
        jax.ShapeDtypeStruct((4, 2, 2048), BF16),
    )
    mixed, attended = pl.pallas_call(
        kernel,
        out_shape=shapes,
        in_specs=[hbm] * 12,
        out_specs=(hbm, hbm),
        scratch_shapes=[
            pltpu.VMEM((16, D), BF16),
            pltpu.VMEM((D,), F32),
            pltpu.VMEM((4, 16), jnp.int32),
            pltpu.VMEM((4, 16), F32),
            pltpu.VMEM((4, 2, 2048), BF16),
            pltpu.VMEM((4, 2, 2, 256), BF16),
            pltpu.VMEM((1, 32), F32),
            pltpu.SMEM((4, 32), jnp.int32),
            pltpu.SMEM((4,), jnp.int32),
            pltpu.VMEM((16, D), BF16),
            pltpu.VMEM((4, 2, 2048), BF16),
            pltpu.VMEM((16, WIDE), BF16),
            pltpu.VMEM((16, WIDE), BF16),
            packed,
            packed,
            packed,
            packed,
            pltpu.VMEM((4 * BATCH, WIDE), BF16),
            pltpu.VMEM((4 * BATCH, WIDE), BF16),
            pltpu.VMEM((128, 1024), BF16),
            pltpu.VMEM((128, 1024), BF16),
            pltpu.VMEM((128, 768), F32),
            pltpu.VMEM((16, WIDE), F32),
            pltpu.VMEM((16, WIDE), F32),
            pltpu.VMEM((2, H, D), BF16),
            pltpu.VMEM((H, D), BF16),
            pltpu.VMEM((128, 2, 64, 256), BF16),
            pltpu.VMEM((4, 64, 256), BF16),
            pltpu.VMEM((64, 2048), F32),
            pltpu.VMEM((4, 64, 256), BF16),
            dma((14,)),
            dma((2,)),
            dma((2,)),
            dma((2,)),
            dma((PEERS // GROUP,)),
            dma((PEERS // GROUP,)),
        ],
        compiler_params=pltpu.CompilerParams(
            collective_id=0, has_side_effects=True, vmem_limit_bytes=56 * 2**20
        ),
        name="decode",
    )(
        tokens, norm_gain, expert_ids.T, gate_weights.T, expert_gate_up.transpose(0, 1, 3, 2), expert_down,
        queries, new_cache, cache_pool, page_table, cache_length,
        sink_logits.reshape(1, 32),
    )
    return pl.pallas_call(
        finish,
        out_shape=shapes,
        in_specs=[vmem] * 2,
        out_specs=(vmem, vmem),
        compiler_params=pltpu.CompilerParams(vmem_limit_bytes=60 * 2**20),
        name="finish",
    )(mixed, attended)


def solution(mesh):
    rows = P(("dp", "ep"))
    placed = (rows, P(), rows, rows, rows, rows, rows, rows, rows, rows, rows, P())
    return jax.shard_map(
        local, mesh=mesh, in_specs=placed, out_specs=(rows, rows), check_vma=False
    )
```

```python
import functools

import jax
import jax.numpy as jnp
from jax import lax
from jax.experimental import pallas as pl
from jax.experimental.pallas import tpu as pltpu
from jax.sharding import PartitionSpec as P

D = 2880
H = 720
WIDE = 3072
QUADS = 6
PEERS = 64
ROWS = 96
GROUP = 16
BATCH = GROUP
EPS = 1e-05
NEG = -1e30
F32 = jnp.float32
BF16 = jnp.bfloat16
MESH = pl.DeviceIdType.MESH
NT = (((1,), (1,)), ((), ()))


def dot(a, b):
    return jnp.dot(a, b, preferred_element_type=F32)


def dot_nt(a, b):
    return lax.dot_general(a, b, NT, preferred_element_type=F32)


def iota(shape, axis):
    return lax.broadcasted_iota(jnp.int32, shape, axis)


def kernel(
    tokens_in, gain_in, ids_in, gates_in, gate_up, down, queries_in, fresh_in, pool, table_in, length_in, sinks_in,
    mixed, attended,
    tokens, gain, ids, gates, queries, fresh, sinks, table, length,
    own, sib, away, landed, back, home, x_rows, o_rows, weight_hi, weight_lo, total, partial,
    gu_v, down_v, pool_v, spread, scores, outs,
    load_sem, pair_send, pair_recv, send_sem, recv_sem, home_recv,
):
    dp = lax.axis_index("dp")
    ep = lax.axis_index("ep")
    x, z = ep // 4, ep % 4
    y, c = dp // 2, dp % 2
    step = 37 - 10 * c

    def peer(i, sign):
        o = (step * i) % PEERS
        px = (x + 4 + sign * (o // 16)) % 4
        py = (y + 4 + sign * ((o // 4) % 4)) % 4
        pz = (z + 4 + sign * (o % 4)) % 4
        return (py * 2 + c, px * 4 + pz)

    sibling = (y * 2 + 1 - c, ep)

    first = [(tokens_in, tokens), (ids_in, ids), (gates_in, gates), (gain_in, gain)]
    later = [(queries_in, queries), (fresh_in, fresh), (sinks_in, sinks), (table_in, table), (length_in, length)]
    first = [pltpu.make_async_copy(a, b, load_sem.at[3 + n]) for n, (a, b) in enumerate(first)]
    later = [pltpu.make_async_copy(a, b, load_sem.at[7 + n]) for n, (a, b) in enumerate(later)]
    for copy in first:
        copy.start()
    pool_copy = pltpu.make_async_copy(pool, pool_v, load_sem.at[0])
    gu_copy = pltpu.make_async_copy(gate_up.at[0], gu_v, load_sem.at[1])
    down_copy = pltpu.make_async_copy(down.at[0], down_v, load_sem.at[2])
    barrier = pltpu.get_barrier_semaphore()
    pl.semaphore_signal(barrier, inc=1, device_id=sibling, device_id_type=MESH)

    def greet(i, carry):
        pl.semaphore_signal(barrier, inc=1, device_id=peer(i, 1), device_id_type=MESH)
        return carry

    lax.fori_loop(1, PEERS, greet, 0)

    for copy in first:
        copy.wait()
    wide = tokens[...].astype(F32)
    mean_square = jnp.sum(wide * wide, axis=1, keepdims=True) * (1.0 / D)
    own[:, 0:D] = (wide * lax.rsqrt(mean_square + EPS) * gain[...].reshape(1, D)).astype(BF16)
    lane = iota((16, 128), 1)
    id_cols = ids[...].T
    gate_cols = gates[...].T
    named = jnp.zeros((16, 128), F32)
    gate_hi = jnp.zeros((16, 128), F32)
    gate_lo = jnp.zeros((16, 128), F32)
    for k in range(4):
        id_k = id_cols[:, k : k + 1]
        gate_k = gate_cols[:, k : k + 1]
        hi_k = gate_k.astype(BF16).astype(F32)
        named = jnp.where(id_k == lane, 1.0, named)
        gate_hi = jnp.where(id_k + 64 == lane, hi_k, gate_hi)
        gate_lo = jnp.where(id_k + 64 == lane, gate_k - hi_k, gate_lo)
    earlier = (iota((16, 16), 1) < iota((16, 16), 0)).astype(BF16)
    rank = dot(earlier, named.astype(BF16))
    code = named * (1.0 + rank)
    tail = own[:, 2816:2944].astype(F32)
    own[:, 2816:2944] = jnp.where(lane < 64, tail, gate_lo).astype(BF16)
    own[:, 2944:3072] = jnp.where(lane < 64, code, gate_hi).astype(BF16)

    pl.semaphore_wait(barrier, PEERS)
    pair = pltpu.make_async_remote_copy(
        src_ref=own, dst_ref=sib, send_sem=pair_send.at[0], recv_sem=pair_recv.at[0],
        device_id=sibling, device_id_type=MESH,
    )
    pair.start()
    for copy in (gu_copy, down_copy, pool_copy, *later):
        copy.start()
    o_rows[:, 2816:3072] = jnp.zeros((4 * BATCH, 256), BF16)
    pair.wait_recv()

    def chunk(n):
        return jnp.concatenate([own[:, n * 128 : n * 128 + 128], sib[:, n * 128 : n * 128 + 128]], axis=0)

    stacked = jnp.concatenate(
        [jnp.concatenate([chunk(4 * q + b) for b in range(4)], axis=0) for q in range(QUADS)], axis=1
    )
    codes23 = jnp.concatenate([chunk(23)] * 4, axis=0)

    def expert_at(i):
        o = (step * i) & 63
        px = (x + (o >> 4)) & 3
        py = (y + ((o >> 2) & 3)) & 3
        pz = (z + (o & 3)) & 3
        return (py * 2 + c) * 8 + ((px * 4 + pz) >> 1)

    def send(i, carry):
        pltpu.make_async_remote_copy(
            src_ref=away.at[i], dst_ref=landed.at[i], send_sem=send_sem.at[0], recv_sem=recv_sem.at[i // GROUP],
            device_id=peer(i, 1), device_id_type=MESH,
        ).start()
        return carry

    for k in range(PEERS // GROUP):
        row = iota((256, 128), 0)
        col = iota((256, 128), 1)
        expert = expert_at(GROUP * k + (row >> 4))
        pick = (expert == col).astype(BF16)
        found = dot_nt(pick, codes23)
        slot = row & 3
        chosen = (
            (((row >> 2) & 3) == (col >> 5))
            & (((col >> 4) & 1) == (slot >> 1))
            & (found == ((slot & 1) + 1).astype(F32))
        )
        packed = dot(chosen.astype(BF16), stacked).astype(BF16)
        for q in range(QUADS):
            away[GROUP * k : GROUP * (k + 1), 16 * q : 16 * q + 16, :] = packed[
                :, 128 * q : 128 * q + 128
            ].reshape(GROUP, 16, 128)
        lax.fori_loop(max(GROUP * k, 1), GROUP * (k + 1), send, 0)
    own_copy = pltpu.make_async_copy(away.at[0], landed.at[0], recv_sem.at[0])
    own_copy.start()

    codes22, codes23 = (
        jnp.concatenate([sib[:, at : at + 128]] * 4 + [own[:, at : at + 128]] * 4, axis=0) for at in (2816, 2944)
    )
    for k in range(PEERS // GROUP):
        row = iota((128, 256), 0)
        col = iota((128, 256), 1)
        wide_row = iota((256, 128), 0)
        wide_col = iota((256, 128), 1)
        expert = expert_at(GROUP * k + (wide_row >> 4))
        pick = (expert == wide_col).astype(BF16)
        pick_gate = (expert + 64 == wide_col).astype(BF16)
        found = dot_nt(codes23, pick)
        slot = col & 3
        chosen = (
            (((col >> 2) & 3) == ((row >> 4) & 3))
            & ((row >> 6) != (slot >> 1))
            & (found == ((slot & 1) + 1).astype(F32))
        )
        weight_hi[:, 256 * k : 256 * k + 256] = jnp.where(chosen, dot_nt(codes23, pick_gate), 0.0).astype(BF16)
        weight_lo[:, 256 * k : 256 * k + 256] = jnp.where(chosen, dot_nt(codes22, pick_gate), 0.0).astype(BF16)

    gu_copy.wait()
    down_copy.wait()

    def outward(at, sem):
        return pltpu.make_async_remote_copy(
            src_ref=away.at[at], dst_ref=landed.at[at], send_sem=send_sem.at[0], recv_sem=recv_sem.at[sem],
            device_id=sibling, device_id_type=MESH,
        )

    def homeward(at, sem):
        return pltpu.make_async_remote_copy(
            src_ref=back.at[at], dst_ref=home.at[at], send_sem=send_sem.at[1], recv_sem=home_recv.at[sem],
            device_id=sibling, device_id_type=MESH,
        )

    def give(i, carry):
        pltpu.make_async_remote_copy(
            src_ref=back.at[i], dst_ref=home.at[i], send_sem=send_sem.at[1], recv_sem=home_recv.at[i // GROUP],
            device_id=peer(i, -1), device_id_type=MESH,
        ).start()
        return carry

    to_row = iota((256, 256), 0)
    to_col = iota((256, 256), 1)
    unpack = (
        ((to_row >> 6) == ((to_col >> 2) & 3))
        & (((to_row >> 2) & 15) == (to_col >> 4))
        & ((to_row & 3) == (to_col & 3))
    ).astype(BF16)
    repack = (
        ((to_col >> 6) == ((to_row >> 2) & 3))
        & (((to_col >> 2) & 15) == (to_row >> 4))
        & ((to_row & 3) == (to_col & 3))
    ).astype(BF16)

    def batch(n, carry):
        start = n * BATCH
        outward(pl.ds(start, GROUP), n).wait_recv()
        for s in range(BATCH // GROUP):
            at = start + s * GROUP
            block = jnp.concatenate(
                [landed[pl.ds(at, GROUP), 16 * q : 16 * q + 16, :].reshape(256, 128) for q in range(QUADS)], axis=1
            )
            flat = dot(unpack, block).astype(BF16)
            for q in range(QUADS):
                for b in range(4):
                    x_rows[64 * s : 64 * s + 64, (4 * q + b) * 128 : (4 * q + b) * 128 + 128] = flat[
                        64 * b : 64 * b + 64, 128 * q : 128 * q + 128
                    ]
        rows = x_rows[:, 0:D]
        gate_value = dot_nt(rows, gu_v[0])
        up_value = dot_nt(rows, gu_v[1])
        hidden = ((up_value + 1.0) * gate_value * jax.nn.sigmoid(1.702 * gate_value)).astype(BF16)
        o_rows[:, 0:D] = dot(hidden, down_v[...]).astype(BF16)
        for s in range(BATCH // GROUP):
            at = start + s * GROUP
            block = jnp.concatenate(
                [
                    jnp.concatenate(
                        [
                            o_rows[64 * s : 64 * s + 64, (4 * q + b) * 128 : (4 * q + b) * 128 + 128]
                            for b in range(4)
                        ],
                        axis=0,
                    )
                    for q in range(QUADS)
                ],
                axis=1,
            )
            flat = dot(repack, block).astype(BF16)
            for q in range(QUADS):
                back[pl.ds(at, GROUP), 16 * q : 16 * q + 16, :] = flat[:, 128 * q : 128 * q + 128].reshape(
                    GROUP, 16, 128
                )
        lax.fori_loop(jnp.maximum(start, 1), start + BATCH, give, 0)
        return carry

    lax.fori_loop(0, PEERS // BATCH, batch, 0)
    own_back = pltpu.make_async_copy(back.at[0], home.at[0], home_recv.at[0])
    own_back.start()

    for copy in later:
        copy.wait()
    def fold(g):
        return (((iota((512, 256), 0) & 63) + 64 * g) == iota((512, 256), 1)).astype(BF16)

    own_head = (iota((64, 512), 1) >> 6) == (iota((64, 512), 0) & 7)
    for g in range(4):
        part = jnp.concatenate([queries[r, :, 512 * g : 512 * g + 512].astype(F32) for r in range(4)], axis=0) * 0.125
        part = jnp.broadcast_to(part[:, None, :], (8, 8, 512)).reshape(64, 512)
        part = jnp.where(own_head, part, 0.0).astype(BF16)
        folded = dot(part, fold(g)).astype(BF16)
        spread[:, 16 * g : 16 * g + 16, :] = folded.reshape(4, 16, 256)
    take = iota((16, 16), 1)
    take_at = iota((16, 16), 0)
    fresh_rows = jnp.concatenate([fresh[r, i].astype(F32) for r in range(4) for i in range(2)], axis=0).astype(BF16)
    fresh_keys = dot(((2 * take_at == take) & (take_at < 8)).astype(BF16), fresh_rows).astype(BF16)
    fresh_values = dot(((2 * take_at + 1 == take) & (take_at < 8)).astype(BF16), fresh_rows).astype(BF16)
    sink_row = iota((64, 32), 0)
    sink_at = (sink_row >> 4) * 8 + (sink_row & 7) == iota((64, 32), 1)
    sink = jnp.sum(jnp.where(sink_at, sinks[...], 0.0), axis=1, keepdims=True)
    pool_copy.wait()

    def request(r, carry):
        query = spread[r]
        limit = length[r]
        fresh_col = iota((64, 16), 1)
        fresh_row = iota((64, 16), 0)
        fresh_ok = ((fresh_col >> 1) == r) & ((fresh_col & 1) <= ((fresh_row >> 3) & 1))
        fresh_scores = jnp.where(fresh_ok, dot_nt(query, fresh_keys), NEG)
        top = jnp.maximum(jnp.max(fresh_scores, axis=1, keepdims=True), sink)
        best = jnp.full((64, 256), NEG, F32)
        for b in range(8):
            keys = jnp.concatenate([pool_v[table[r, 4 * b + i], 0] for i in range(4)], axis=0)
            block = dot_nt(query, keys)
            block = jnp.where(iota((64, 256), 1) + 256 * b < limit, block, NEG)
            scores[:, 256 * b : 256 * b + 256] = block
            best = jnp.maximum(best, block)
        top = jnp.maximum(top, jnp.max(best, axis=1, keepdims=True))
        fresh_exp = jnp.where(fresh_ok, jnp.exp(fresh_scores - top), 0.0)
        result = dot(fresh_exp.astype(BF16), fresh_values)
        summed = jnp.zeros((64, 256), F32)
        for b in range(8):
            ok = iota((64, 256), 1) + 256 * b < limit
            block = jnp.where(ok, jnp.exp(scores[:, 256 * b : 256 * b + 256] - top), 0.0)
            summed = summed + block
            values = jnp.concatenate([pool_v[table[r, 4 * b + i], 1] for i in range(4)], axis=0)
            result = result + dot(block.astype(BF16), values)
        denominator = (
            jnp.exp(sink - top)
            + jnp.sum(fresh_exp, axis=1, keepdims=True)
            + jnp.sum(summed, axis=1, keepdims=True)
        )
        outs[r] = (result / denominator).astype(BF16)
        return carry

    lax.fori_loop(0, 4, request, 0)
    for g in range(4):
        part = outs[:, 16 * g : 16 * g + 16, :].reshape(64, 256)
        part = jnp.where(own_head, dot_nt(part, fold(g)), 0.0)
        part = jnp.sum(part.reshape(8, 8, 512), axis=1)
        for r in range(4):
            attended[r, :, 512 * g : 512 * g + 512] = part[2 * r : 2 * r + 2].astype(BF16)

    swap = pltpu.make_async_remote_copy(
        src_ref=total.at[0], dst_ref=partial, send_sem=pair_send.at[1], recv_sem=pair_recv.at[1],
        device_id=sibling, device_id_type=MESH,
    )
    for k in range(PEERS // GROUP):
        homeward(pl.ds(GROUP * k, GROUP), k).wait_recv()
        block = jnp.concatenate(
            [home[GROUP * k : GROUP * (k + 1), 16 * q : 16 * q + 16, :].reshape(256, 128) for q in range(QUADS)],
            axis=1,
        )
        for half in range(2):
            at = (slice(64 * half, 64 * half + 64), slice(256 * k, 256 * k + 256))
            here = dot(weight_hi[at], block) + dot(weight_lo[at], block)
            if k:
                here = here + total[half]
            total[half] = here
            if half == 0 and k == PEERS // GROUP - 1:
                swap.start()

    outward(pl.ds(1, PEERS - 1), 0).wait_send()
    homeward(pl.ds(1, PEERS - 1), 0).wait_send()
    pair.wait_send()
    swap.wait()
    for n in range(23):
        q, b = n // 4, n % 4
        width = min(128, D - 128 * n)
        at = slice(128 * n, 128 * n + width)
        part = (slice(16 * b, 16 * b + 16), slice(128 * q, 128 * q + width))
        mixed[:, at] = (tokens[:, at].astype(F32) + total[(1, *part)] + partial[part]).astype(BF16)


def finish(mixed_in, attended_in, mixed, attended, sem):
    copies = [
        pltpu.make_async_copy(mixed_in, mixed, sem.at[0]),
        pltpu.make_async_copy(attended_in, attended, sem.at[1]),
    ]
    for copy in copies:
        copy.start()
    for copy in copies:
        copy.wait()


def local(
    tokens, norm_gain, expert_ids, gate_weights, expert_gate_up, expert_down,
    queries, new_cache, cache_pool, page_table, cache_length, sink_logits,
):
    hbm = pl.BlockSpec(memory_space=pl.ANY)
    vmem = pl.BlockSpec(memory_space=pltpu.VMEM)
    dma = pltpu.SemaphoreType.DMA
    packed = pltpu.VMEM((PEERS, ROWS, 128), BF16)
    shapes = (
        jax.ShapeDtypeStruct((16, D), BF16),
        jax.ShapeDtypeStruct((4, 2, 2048), BF16),
    )
    mixed, attended = pl.pallas_call(
        kernel,
        out_shape=(pltpu.VMEM((16, D), BF16), pltpu.VMEM((4, 2, 2048), BF16)),
        in_specs=[hbm] * 12,
        out_specs=(vmem, vmem),
        scratch_shapes=[
            pltpu.VMEM((16, D), BF16),
            pltpu.VMEM((D,), F32),
            pltpu.VMEM((4, 16), jnp.int32),
            pltpu.VMEM((4, 16), F32),
            pltpu.VMEM((4, 2, 2048), BF16),
            pltpu.VMEM((4, 2, 2, 256), BF16),
            pltpu.VMEM((1, 32), F32),
            pltpu.SMEM((4, 32), jnp.int32),
            pltpu.SMEM((4,), jnp.int32),
            pltpu.VMEM((16, WIDE), BF16),
            pltpu.VMEM((16, WIDE), BF16),
            packed,
            packed,
            packed,
            packed,
            pltpu.VMEM((4 * BATCH, WIDE), BF16),
            pltpu.VMEM((4 * BATCH, WIDE), BF16),
            pltpu.VMEM((128, 1024), BF16),
            pltpu.VMEM((128, 1024), BF16),
            pltpu.VMEM((2, 64, 768), F32),
            pltpu.VMEM((64, 768), F32),
            pltpu.VMEM((2, H, D), BF16),
            pltpu.VMEM((H, D), BF16),
            pltpu.VMEM((128, 2, 64, 256), BF16),
            pltpu.VMEM((4, 64, 256), BF16),
            pltpu.VMEM((64, 2048), F32),
            pltpu.VMEM((4, 64, 256), BF16),
            dma((12,)),
            dma((2,)),
            dma((2,)),
            dma((2,)),
            dma((PEERS // GROUP,)),
            dma((PEERS // GROUP,)),
        ],
        compiler_params=pltpu.CompilerParams(
            collective_id=0, has_side_effects=True, vmem_limit_bytes=56 * 2**20
        ),
        name="decode",
    )(
        tokens, norm_gain, expert_ids.T, gate_weights.T, expert_gate_up.transpose(0, 1, 3, 2), expert_down,
        queries, new_cache, cache_pool, page_table, cache_length,
        sink_logits.reshape(1, 32),
    )
    return pl.pallas_call(
        finish,
        out_shape=shapes,
        in_specs=[vmem] * 2,
        out_specs=(hbm, hbm),
        scratch_shapes=[dma((2,))],
        compiler_params=pltpu.CompilerParams(vmem_limit_bytes=4 * 2**20),
        name="finish",
    )(mixed, attended)


def solution(mesh):
    rows = P(("dp", "ep"))
    placed = (rows, P(), rows, rows, rows, rows, rows, rows, rows, rows, rows, P())
    return jax.shard_map(
        local, mesh=mesh, in_specs=placed, out_specs=(rows, rows), check_vma=False
    )
```

```python
import functools

import jax
import jax.numpy as jnp
from jax import lax
from jax.experimental import pallas as pl
from jax.experimental.pallas import tpu as pltpu
from jax.sharding import PartitionSpec as P

D = 2880
H = 720
WIDE = 3072
QUADS = 6
PEERS = 64
ROWS = 96
GROUP = 16
BATCH = GROUP
EPS = 1e-05
NEG = -1e30
F32 = jnp.float32
BF16 = jnp.bfloat16
MESH = pl.DeviceIdType.MESH
NT = (((1,), (1,)), ((), ()))


def dot(a, b):
    return jnp.dot(a, b, preferred_element_type=F32)


def dot_nt(a, b):
    return lax.dot_general(a, b, NT, preferred_element_type=F32)


def iota(shape, axis):
    return lax.broadcasted_iota(jnp.int32, shape, axis)


def kernel(
    tokens_in, gain_in, ids_in, gates_in, gate_up, down, queries_in, fresh_in, pool, table_in, length_in, sinks_in,
    mixed, attended,
    tokens, gain, ids, gates, queries, fresh, sinks, table, length,
    own, sib, away, landed, back, home, x_rows, o_rows, picks, weights, total, partial,
    gu_v, down_v, pool_v, spread, scores, outs,
    load_sem, pair_send, pair_recv, send_sem, recv_sem, home_recv,
):
    dp = lax.axis_index("dp")
    ep = lax.axis_index("ep")
    x, z = ep // 4, ep % 4
    y, c = dp // 2, dp % 2
    step = 37 - 10 * c

    def peer(i, sign):
        o = (step * i) % PEERS
        px = (x + 4 + sign * (o // 16)) % 4
        py = (y + 4 + sign * ((o // 4) % 4)) % 4
        pz = (z + 4 + sign * (o % 4)) % 4
        return (py * 2 + c, px * 4 + pz)

    sibling = (y * 2 + 1 - c, ep)

    first = [(tokens_in, tokens), (ids_in, ids), (gates_in, gates), (gain_in, gain)]
    later = [(queries_in, queries), (fresh_in, fresh), (sinks_in, sinks), (table_in, table), (length_in, length)]
    first = [pltpu.make_async_copy(a, b, load_sem.at[3 + n]) for n, (a, b) in enumerate(first)]
    later = [pltpu.make_async_copy(a, b, load_sem.at[7 + n]) for n, (a, b) in enumerate(later)]
    for copy in first:
        copy.start()
    pool_copy = pltpu.make_async_copy(pool, pool_v, load_sem.at[0])
    gu_copy = pltpu.make_async_copy(gate_up.at[0], gu_v, load_sem.at[1])
    down_copy = pltpu.make_async_copy(down.at[0], down_v, load_sem.at[2])
    barrier = pltpu.get_barrier_semaphore()
    pl.semaphore_signal(barrier, inc=1, device_id=sibling, device_id_type=MESH)

    def greet(i, carry):
        pl.semaphore_signal(barrier, inc=1, device_id=peer(i, 1), device_id_type=MESH)
        return carry

    lax.fori_loop(1, PEERS, greet, 0)

    for copy in first:
        copy.wait()
    wide = tokens[...].astype(F32)
    mean_square = jnp.sum(wide * wide, axis=1, keepdims=True) * (1.0 / D)
    own[:, 0:D] = (wide * lax.rsqrt(mean_square + EPS) * gain[...].reshape(1, D)).astype(BF16)
    lane = iota((16, 128), 1)
    id_cols = ids[...].T
    gate_cols = gates[...].T
    named = jnp.zeros((16, 128), F32)
    gate_hi = jnp.zeros((16, 128), F32)
    gate_lo = jnp.zeros((16, 128), F32)
    for k in range(4):
        id_k = id_cols[:, k : k + 1]
        gate_k = gate_cols[:, k : k + 1]
        hi_k = gate_k.astype(BF16).astype(F32)
        named = jnp.where(id_k == lane, 1.0, named)
        gate_hi = jnp.where(id_k + 64 == lane, hi_k, gate_hi)
        gate_lo = jnp.where(id_k + 64 == lane, gate_k - hi_k, gate_lo)
    earlier = (iota((16, 16), 1) < iota((16, 16), 0)).astype(BF16)
    rank = dot(earlier, named.astype(BF16))
    code = named * (1.0 + rank)
    tail = own[:, 2816:2944].astype(F32)
    own[:, 2816:2944] = jnp.where(lane < 64, tail, gate_lo).astype(BF16)
    own[:, 2944:3072] = jnp.where(lane < 64, code, gate_hi).astype(BF16)

    pl.semaphore_wait(barrier, PEERS)
    pair = pltpu.make_async_remote_copy(
        src_ref=own, dst_ref=sib, send_sem=pair_send.at[0], recv_sem=pair_recv.at[0],
        device_id=sibling, device_id_type=MESH,
    )
    pair.start()
    for copy in (gu_copy, down_copy, pool_copy, *later):
        copy.start()
    o_rows[:, 2816:3072] = jnp.zeros((4 * BATCH, 256), BF16)
    def expert_at(i):
        o = (step * i) & 63
        px = (x + (o >> 4)) & 3
        py = (y + ((o >> 2) & 3)) & 3
        pz = (z + (o & 3)) & 3
        return (py * 2 + c) * 8 + ((px * 4 + pz) >> 1)

    row = iota((256, 128), 0)
    col = iota((256, 128), 1)
    for k in range(PEERS // GROUP):
        picks[k] = (expert_at(GROUP * k + (row >> 4)) == col).astype(BF16)
    pair.wait_recv()

    def chunk(n):
        return jnp.concatenate([own[:, n * 128 : n * 128 + 128], sib[:, n * 128 : n * 128 + 128]], axis=0)

    stacked = jnp.concatenate(
        [jnp.concatenate([chunk(4 * q + b) for b in range(4)], axis=0) for q in range(QUADS)], axis=1
    )
    codes23 = jnp.concatenate([chunk(23)] * 4, axis=0)

    def send(i, carry):
        pltpu.make_async_remote_copy(
            src_ref=away.at[i], dst_ref=landed.at[i], send_sem=send_sem.at[0], recv_sem=recv_sem.at[i // GROUP],
            device_id=peer(i, 1), device_id_type=MESH,
        ).start()
        return carry

    for k in range(PEERS // GROUP):
        row = iota((256, 128), 0)
        col = iota((256, 128), 1)
        found = dot_nt(picks[k], codes23)
        slot = row & 3
        chosen = (
            (((row >> 2) & 3) == (col >> 5))
            & (((col >> 4) & 1) == (slot >> 1))
            & (found == ((slot & 1) + 1).astype(F32))
        )
        packed = dot(chosen.astype(BF16), stacked).astype(BF16)
        for q in range(QUADS):
            away[GROUP * k : GROUP * (k + 1), 16 * q : 16 * q + 16, :] = packed[
                :, 128 * q : 128 * q + 128
            ].reshape(GROUP, 16, 128)
        lax.fori_loop(max(GROUP * k, 1), GROUP * (k + 1), send, 0)
    own_copy = pltpu.make_async_copy(away.at[0], landed.at[0], recv_sem.at[0])
    own_copy.start()

    codes22, codes23 = (
        jnp.concatenate([sib[:, at : at + 128]] * 4 + [own[:, at : at + 128]] * 4, axis=0) for at in (2816, 2944)
    )
    for k in range(PEERS // GROUP):
        row = iota((128, 256), 0)
        col = iota((128, 256), 1)
        wide_row = iota((256, 128), 0)
        wide_col = iota((256, 128), 1)
        expert = expert_at(GROUP * k + (wide_row >> 4))
        pick_gate = (expert + 64 == wide_col).astype(BF16)
        found = dot_nt(codes23, picks[k])
        slot = col & 3
        chosen = (
            (((col >> 2) & 3) == ((row >> 4) & 3))
            & ((row >> 6) != (slot >> 1))
            & (found == ((slot & 1) + 1).astype(F32))
        )
        for part, codes in enumerate((codes23, codes22)):
            weight = jnp.where(chosen, dot_nt(codes, pick_gate), 0.0).astype(BF16)
            for half in range(2):
                at = 128 * half + 64 * part
                weights[at : at + 64, 256 * k : 256 * k + 256] = weight[64 * half : 64 * half + 64]

    gu_copy.wait()
    down_copy.wait()

    def outward(at, sem):
        return pltpu.make_async_remote_copy(
            src_ref=away.at[at], dst_ref=landed.at[at], send_sem=send_sem.at[0], recv_sem=recv_sem.at[sem],
            device_id=sibling, device_id_type=MESH,
        )

    def homeward(at, sem):
        return pltpu.make_async_remote_copy(
            src_ref=back.at[at], dst_ref=home.at[at], send_sem=send_sem.at[1], recv_sem=home_recv.at[sem],
            device_id=sibling, device_id_type=MESH,
        )

    def give(i, carry):
        pltpu.make_async_remote_copy(
            src_ref=back.at[i], dst_ref=home.at[i], send_sem=send_sem.at[1], recv_sem=home_recv.at[i // GROUP],
            device_id=peer(i, -1), device_id_type=MESH,
        ).start()
        return carry

    to_row = iota((256, 256), 0)
    to_col = iota((256, 256), 1)
    unpack = (
        ((to_row >> 6) == ((to_col >> 2) & 3))
        & (((to_row >> 2) & 15) == (to_col >> 4))
        & ((to_row & 3) == (to_col & 3))
    ).astype(BF16)
    repack = (
        ((to_col >> 6) == ((to_row >> 2) & 3))
        & (((to_col >> 2) & 15) == (to_row >> 4))
        & ((to_row & 3) == (to_col & 3))
    ).astype(BF16)

    def batch(n, carry):
        start = n * BATCH
        outward(pl.ds(start, GROUP), n).wait_recv()
        for s in range(BATCH // GROUP):
            at = start + s * GROUP
            block = jnp.concatenate(
                [landed[pl.ds(at, GROUP), 16 * q : 16 * q + 16, :].reshape(256, 128) for q in range(QUADS)], axis=1
            )
            flat = dot(unpack, block).astype(BF16)
            for q in range(QUADS):
                for b in range(4):
                    x_rows[64 * s : 64 * s + 64, (4 * q + b) * 128 : (4 * q + b) * 128 + 128] = flat[
                        64 * b : 64 * b + 64, 128 * q : 128 * q + 128
                    ]
        rows = x_rows[:, 0:D]
        gate_value = dot_nt(rows, gu_v[0])
        up_value = dot_nt(rows, gu_v[1])
        hidden = ((up_value + 1.0) * gate_value * jax.nn.sigmoid(1.702 * gate_value)).astype(BF16)
        o_rows[:, 0:D] = dot(hidden, down_v[...]).astype(BF16)
        for s in range(BATCH // GROUP):
            at = start + s * GROUP
            block = jnp.concatenate(
                [
                    jnp.concatenate(
                        [
                            o_rows[64 * s : 64 * s + 64, (4 * q + b) * 128 : (4 * q + b) * 128 + 128]
                            for b in range(4)
                        ],
                        axis=0,
                    )
                    for q in range(QUADS)
                ],
                axis=1,
            )
            flat = dot(repack, block).astype(BF16)
            for q in range(QUADS):
                back[pl.ds(at, GROUP), 16 * q : 16 * q + 16, :] = flat[:, 128 * q : 128 * q + 128].reshape(
                    GROUP, 16, 128
                )
        lax.fori_loop(jnp.maximum(start, 1), start + BATCH, give, 0)
        return carry

    lax.fori_loop(0, PEERS // BATCH, batch, 0)
    own_back = pltpu.make_async_copy(back.at[0], home.at[0], home_recv.at[0])
    own_back.start()

    for copy in later:
        copy.wait()
    def fold(g):
        return (((iota((512, 256), 0) & 63) + 64 * g) == iota((512, 256), 1)).astype(BF16)

    own_head = (iota((64, 512), 1) >> 6) == (iota((64, 512), 0) & 7)
    for g in range(4):
        part = jnp.concatenate([queries[r, :, 512 * g : 512 * g + 512].astype(F32) for r in range(4)], axis=0) * 0.125
        part = jnp.broadcast_to(part[:, None, :], (8, 8, 512)).reshape(64, 512)
        part = jnp.where(own_head, part, 0.0).astype(BF16)
        folded = dot(part, fold(g)).astype(BF16)
        spread[:, 16 * g : 16 * g + 16, :] = folded.reshape(4, 16, 256)
    take = iota((16, 16), 1)
    take_at = iota((16, 16), 0)
    fresh_rows = jnp.concatenate([fresh[r, i].astype(F32) for r in range(4) for i in range(2)], axis=0).astype(BF16)
    fresh_keys = dot(((2 * take_at == take) & (take_at < 8)).astype(BF16), fresh_rows).astype(BF16)
    fresh_values = dot(((2 * take_at + 1 == take) & (take_at < 8)).astype(BF16), fresh_rows).astype(BF16)
    sink_row = iota((64, 32), 0)
    sink_at = (sink_row >> 4) * 8 + (sink_row & 7) == iota((64, 32), 1)
    sink = jnp.sum(jnp.where(sink_at, sinks[...], 0.0), axis=1, keepdims=True)
    pool_copy.wait()

    def request(r, carry):
        query = spread[r]
        limit = length[r]
        fresh_col = iota((64, 16), 1)
        fresh_row = iota((64, 16), 0)
        fresh_ok = ((fresh_col >> 1) == r) & ((fresh_col & 1) <= ((fresh_row >> 3) & 1))
        fresh_scores = jnp.where(fresh_ok, dot_nt(query, fresh_keys), NEG)
        top = jnp.maximum(jnp.max(fresh_scores, axis=1, keepdims=True), sink)
        best = jnp.full((64, 256), NEG, F32)
        for b in range(8):
            keys = jnp.concatenate([pool_v[table[r, 4 * b + i], 0] for i in range(4)], axis=0)
            block = dot_nt(query, keys)
            block = jnp.where(iota((64, 256), 1) + 256 * b < limit, block, NEG)
            scores[:, 256 * b : 256 * b + 256] = block
            best = jnp.maximum(best, block)
        top = jnp.maximum(top, jnp.max(best, axis=1, keepdims=True))
        fresh_exp = jnp.where(fresh_ok, jnp.exp(fresh_scores - top), 0.0)
        result = dot(fresh_exp.astype(BF16), fresh_values)
        summed = jnp.zeros((64, 256), F32)
        for b in range(8):
            ok = iota((64, 256), 1) + 256 * b < limit
            block = jnp.where(ok, jnp.exp(scores[:, 256 * b : 256 * b + 256] - top), 0.0)
            summed = summed + block
            values = jnp.concatenate([pool_v[table[r, 4 * b + i], 1] for i in range(4)], axis=0)
            result = result + dot(block.astype(BF16), values)
        denominator = (
            jnp.exp(sink - top)
            + jnp.sum(fresh_exp, axis=1, keepdims=True)
            + jnp.sum(summed, axis=1, keepdims=True)
        )
        outs[r] = (result / denominator).astype(BF16)
        return carry

    lax.fori_loop(0, 4, request, 0)
    for g in range(4):
        part = outs[:, 16 * g : 16 * g + 16, :].reshape(64, 256)
        part = jnp.where(own_head, dot_nt(part, fold(g)), 0.0)
        part = jnp.sum(part.reshape(8, 8, 512), axis=1)
        for r in range(4):
            attended[r, :, 512 * g : 512 * g + 512] = part[2 * r : 2 * r + 2].astype(BF16)

    swap = pltpu.make_async_remote_copy(
        src_ref=total.at[0], dst_ref=partial, send_sem=pair_send.at[1], recv_sem=pair_recv.at[1],
        device_id=sibling, device_id_type=MESH,
    )
    for k in range(PEERS // GROUP):
        homeward(pl.ds(GROUP * k, GROUP), k).wait_recv()
        block = jnp.concatenate(
            [home[GROUP * k : GROUP * (k + 1), 16 * q : 16 * q + 16, :].reshape(256, 128) for q in range(QUADS)],
            axis=1,
        )
        for half in range(2):
            both = dot(weights[128 * half : 128 * half + 128, 256 * k : 256 * k + 256], block)
            here = both[0:64] + both[64:128]
            if k:
                here = here + total[half]
            total[half] = here
            if half == 0 and k == PEERS // GROUP - 1:
                swap.start()

    outward(pl.ds(1, PEERS - 1), 0).wait_send()
    homeward(pl.ds(1, PEERS - 1), 0).wait_send()
    pair.wait_send()
    swap.wait()
    for n in range(23):
        q, b = n // 4, n % 4
        width = min(128, D - 128 * n)
        at = slice(128 * n, 128 * n + width)
        part = (slice(16 * b, 16 * b + 16), slice(128 * q, 128 * q + width))
        mixed[:, at] = (tokens[:, at].astype(F32) + total[(1, *part)] + partial[part]).astype(BF16)


def finish(mixed_in, attended_in, mixed, attended, sem):
    copies = [
        pltpu.make_async_copy(mixed_in, mixed, sem.at[0]),
        pltpu.make_async_copy(attended_in, attended, sem.at[1]),
    ]
    for copy in copies:
        copy.start()
    for copy in copies:
        copy.wait()


def local(
    tokens, norm_gain, expert_ids, gate_weights, expert_gate_up, expert_down,
    queries, new_cache, cache_pool, page_table, cache_length, sink_logits,
):
    hbm = pl.BlockSpec(memory_space=pl.ANY)
    vmem = pl.BlockSpec(memory_space=pltpu.VMEM)
    dma = pltpu.SemaphoreType.DMA
    packed = pltpu.VMEM((PEERS, ROWS, 128), BF16)
    shapes = (
        jax.ShapeDtypeStruct((16, D), BF16),
        jax.ShapeDtypeStruct((4, 2, 2048), BF16),
    )
    mixed, attended = pl.pallas_call(
        kernel,
        out_shape=(pltpu.VMEM((16, D), BF16), pltpu.VMEM((4, 2, 2048), BF16)),
        in_specs=[hbm] * 12,
        out_specs=(vmem, vmem),
        scratch_shapes=[
            pltpu.VMEM((16, D), BF16),
            pltpu.VMEM((D,), F32),
            pltpu.VMEM((4, 16), jnp.int32),
            pltpu.VMEM((4, 16), F32),
            pltpu.VMEM((4, 2, 2048), BF16),
            pltpu.VMEM((4, 2, 2, 256), BF16),
            pltpu.VMEM((1, 32), F32),
            pltpu.SMEM((4, 32), jnp.int32),
            pltpu.SMEM((4,), jnp.int32),
            pltpu.VMEM((16, WIDE), BF16),
            pltpu.VMEM((16, WIDE), BF16),
            packed,
            packed,
            packed,
            packed,
            pltpu.VMEM((4 * BATCH, WIDE), BF16),
            pltpu.VMEM((4 * BATCH, WIDE), BF16),
            pltpu.VMEM((4, 256, 128), BF16),
            pltpu.VMEM((256, 1024), BF16),
            pltpu.VMEM((2, 64, 768), F32),
            pltpu.VMEM((64, 768), F32),
            pltpu.VMEM((2, H, D), BF16),
            pltpu.VMEM((H, D), BF16),
            pltpu.VMEM((128, 2, 64, 256), BF16),
            pltpu.VMEM((4, 64, 256), BF16),
            pltpu.VMEM((64, 2048), F32),
            pltpu.VMEM((4, 64, 256), BF16),
            dma((12,)),
            dma((2,)),
            dma((2,)),
            dma((2,)),
            dma((PEERS // GROUP,)),
            dma((PEERS // GROUP,)),
        ],
        compiler_params=pltpu.CompilerParams(
            collective_id=0, has_side_effects=True, vmem_limit_bytes=56 * 2**20
        ),
        name="decode",
    )(
        tokens, norm_gain, expert_ids.T, gate_weights.T, expert_gate_up.transpose(0, 1, 3, 2), expert_down,
        queries, new_cache, cache_pool, page_table, cache_length,
        sink_logits.reshape(1, 32),
    )
    return pl.pallas_call(
        finish,
        out_shape=shapes,
        in_specs=[vmem] * 2,
        out_specs=(hbm, hbm),
        scratch_shapes=[dma((2,))],
        compiler_params=pltpu.CompilerParams(vmem_limit_bytes=4 * 2**20),
        name="finish",
    )(mixed, attended)


def solution(mesh):
    rows = P(("dp", "ep"))
    placed = (rows, P(), rows, rows, rows, rows, rows, rows, rows, rows, rows, P())
    return jax.shard_map(
        local, mesh=mesh, in_specs=placed, out_specs=(rows, rows), check_vma=False
    )
```

```python
import functools

import jax
import jax.numpy as jnp
from jax import lax
from jax.experimental import pallas as pl
from jax.experimental.pallas import tpu as pltpu
from jax.sharding import PartitionSpec as P

D = 2880
H = 720
WIDE = 3072
QUADS = 6
PEERS = 64
ROWS = 96
GROUP = 16
BATCH = GROUP
EPS = 1e-05
NEG = -1e30
F32 = jnp.float32
BF16 = jnp.bfloat16
MESH = pl.DeviceIdType.MESH
NT = (((1,), (1,)), ((), ()))


def dot(a, b):
    return jnp.dot(a, b, preferred_element_type=F32)


def dot_nt(a, b):
    return lax.dot_general(a, b, NT, preferred_element_type=F32)


def iota(shape, axis):
    return lax.broadcasted_iota(jnp.int32, shape, axis)


def kernel(
    tokens_in, gain_in, ids_in, gates_in, gate_up, down, queries_in, fresh_in, pool, table_in, length_in, sinks_in,
    mixed, attended,
    tokens, gain, ids, gates, queries, fresh, sinks, table, length,
    own, sib, away, landed, back, home, x_rows, o_rows, weights, total, given, partial,
    gu_v, down_v, pool_v, spread, scores, outs,
    load_sem, pair_send, pair_recv, send_sem, recv_sem, home_recv,
):
    dp = lax.axis_index("dp")
    ep = lax.axis_index("ep")
    x, z = ep // 4, ep % 4
    y, c = dp // 2, dp % 2
    step = 37 - 10 * c

    def peer(i, sign):
        o = (step * i) % PEERS
        px = (x + 4 + sign * (o // 16)) % 4
        py = (y + 4 + sign * ((o // 4) % 4)) % 4
        pz = (z + 4 + sign * (o % 4)) % 4
        return (py * 2 + c, px * 4 + pz)

    sibling = (y * 2 + 1 - c, ep)

    first = [(tokens_in, tokens), (ids_in, ids), (gates_in, gates), (gain_in, gain)]
    later = [(queries_in, queries), (fresh_in, fresh), (sinks_in, sinks), (table_in, table), (length_in, length)]
    first = [pltpu.make_async_copy(a, b, load_sem.at[3 + n]) for n, (a, b) in enumerate(first)]
    later = [pltpu.make_async_copy(a, b, load_sem.at[7 + n]) for n, (a, b) in enumerate(later)]
    for copy in first:
        copy.start()
    pool_copy = pltpu.make_async_copy(pool, pool_v, load_sem.at[0])
    gu_copy = pltpu.make_async_copy(gate_up.at[0], gu_v, load_sem.at[1])
    down_copy = pltpu.make_async_copy(down.at[0], down_v, load_sem.at[2])
    barrier = pltpu.get_barrier_semaphore()
    pl.semaphore_signal(barrier, inc=1, device_id=sibling, device_id_type=MESH)

    def greet(i, carry):
        pl.semaphore_signal(barrier, inc=1, device_id=peer(i, 1), device_id_type=MESH)
        return carry

    lax.fori_loop(1, PEERS, greet, 0)

    for copy in first:
        copy.wait()
    wide = tokens[...].astype(F32)
    mean_square = jnp.sum(wide * wide, axis=1, keepdims=True) * (1.0 / D)
    own[:, 0:D] = (wide * lax.rsqrt(mean_square + EPS) * gain[...].reshape(1, D)).astype(BF16)
    lane = iota((16, 128), 1)
    id_cols = ids[...].T
    gate_cols = gates[...].T
    named = jnp.zeros((16, 128), F32)
    gate_hi = jnp.zeros((16, 128), F32)
    gate_lo = jnp.zeros((16, 128), F32)
    for k in range(4):
        id_k = id_cols[:, k : k + 1]
        gate_k = gate_cols[:, k : k + 1]
        hi_k = gate_k.astype(BF16).astype(F32)
        named = jnp.where(id_k == lane, 1.0, named)
        gate_hi = jnp.where(id_k + 64 == lane, hi_k, gate_hi)
        gate_lo = jnp.where(id_k + 64 == lane, gate_k - hi_k, gate_lo)
    earlier = (iota((16, 16), 1) < iota((16, 16), 0)).astype(BF16)
    rank = dot(earlier, named.astype(BF16))
    code = named * (1.0 + rank)
    tail = own[:, 2816:2944].astype(F32)
    own[:, 2816:2944] = jnp.where(lane < 64, tail, gate_lo).astype(BF16)
    own[:, 2944:3072] = jnp.where(lane < 64, code, gate_hi).astype(BF16)

    pl.semaphore_wait(barrier, PEERS)
    pair = pltpu.make_async_remote_copy(
        src_ref=own, dst_ref=sib, send_sem=pair_send.at[0], recv_sem=pair_recv.at[0],
        device_id=sibling, device_id_type=MESH,
    )
    pair.start()
    for copy in (gu_copy, down_copy, pool_copy, *later):
        copy.start()
    o_rows[:, 2816:3072] = jnp.zeros((4 * BATCH, 256), BF16)
    pair.wait_recv()

    def chunk(n):
        return jnp.concatenate([own[:, n * 128 : n * 128 + 128], sib[:, n * 128 : n * 128 + 128]], axis=0)

    stacked = jnp.concatenate(
        [jnp.concatenate([chunk(4 * q + b) for b in range(4)], axis=0) for q in range(QUADS)], axis=1
    )
    codes23 = jnp.concatenate([chunk(23)] * 4, axis=0)

    def expert_at(i):
        o = (step * i) & 63
        px = (x + (o >> 4)) & 3
        py = (y + ((o >> 2) & 3)) & 3
        pz = (z + (o & 3)) & 3
        return (py * 2 + c) * 8 + ((px * 4 + pz) >> 1)

    def send(i, carry):
        pltpu.make_async_remote_copy(
            src_ref=away.at[i], dst_ref=landed.at[i], send_sem=send_sem.at[0], recv_sem=recv_sem.at[i // GROUP],
            device_id=peer(i, 1), device_id_type=MESH,
        ).start()
        return carry

    for k in range(PEERS // GROUP):
        row = iota((256, 128), 0)
        col = iota((256, 128), 1)
        expert = expert_at(GROUP * k + (row >> 4))
        pick = (expert == col).astype(BF16)
        found = dot_nt(pick, codes23)
        slot = row & 3
        chosen = (
            (((row >> 2) & 3) == (col >> 5))
            & (((col >> 4) & 1) == (slot >> 1))
            & (found == ((slot & 1) + 1).astype(F32))
        )
        packed = dot(chosen.astype(BF16), stacked).astype(BF16)
        for q in range(QUADS):
            away[GROUP * k : GROUP * (k + 1), 16 * q : 16 * q + 16, :] = packed[
                :, 128 * q : 128 * q + 128
            ].reshape(GROUP, 16, 128)
        lax.fori_loop(max(GROUP * k, 1), GROUP * (k + 1), send, 0)
    own_copy = pltpu.make_async_copy(away.at[0], landed.at[0], recv_sem.at[0])
    own_copy.start()

    codes22, codes23 = (
        jnp.concatenate([sib[:, at : at + 128]] * 4 + [own[:, at : at + 128]] * 4, axis=0) for at in (2816, 2944)
    )
    for k in range(PEERS // GROUP):
        row = iota((128, 256), 0)
        col = iota((128, 256), 1)
        wide_row = iota((256, 128), 0)
        wide_col = iota((256, 128), 1)
        expert = expert_at(GROUP * k + (wide_row >> 4))
        pick = (expert == wide_col).astype(BF16)
        pick_gate = (expert + 64 == wide_col).astype(BF16)
        found = dot_nt(codes23, pick)
        slot = col & 3
        chosen = (
            (((col >> 2) & 3) == ((row >> 4) & 3))
            & ((row >> 6) != (slot >> 1))
            & (found == ((slot & 1) + 1).astype(F32))
        )
        for part, codes in enumerate((codes23, codes22)):
            weight = jnp.where(chosen, dot_nt(codes, pick_gate), 0.0).astype(BF16)
            for half in range(2):
                at = 128 * half + 64 * part
                weights[at : at + 64, 256 * k : 256 * k + 256] = weight[64 * half : 64 * half + 64]

    gu_copy.wait()
    down_copy.wait()

    def outward(at, sem):
        return pltpu.make_async_remote_copy(
            src_ref=away.at[at], dst_ref=landed.at[at], send_sem=send_sem.at[0], recv_sem=recv_sem.at[sem],
            device_id=sibling, device_id_type=MESH,
        )

    def homeward(at, sem):
        return pltpu.make_async_remote_copy(
            src_ref=back.at[at], dst_ref=home.at[at], send_sem=send_sem.at[1], recv_sem=home_recv.at[sem],
            device_id=sibling, device_id_type=MESH,
        )

    def give(i, carry):
        pltpu.make_async_remote_copy(
            src_ref=back.at[i], dst_ref=home.at[i], send_sem=send_sem.at[1], recv_sem=home_recv.at[i // GROUP],
            device_id=peer(i, -1), device_id_type=MESH,
        ).start()
        return carry

    to_row = iota((256, 256), 0)
    to_col = iota((256, 256), 1)
    unpack = (
        ((to_row >> 6) == ((to_col >> 2) & 3))
        & (((to_row >> 2) & 15) == (to_col >> 4))
        & ((to_row & 3) == (to_col & 3))
    ).astype(BF16)
    repack = (
        ((to_col >> 6) == ((to_row >> 2) & 3))
        & (((to_col >> 2) & 15) == (to_row >> 4))
        & ((to_row & 3) == (to_col & 3))
    ).astype(BF16)

    def batch(n, carry):
        start = n * BATCH
        outward(pl.ds(start, GROUP), n).wait_recv()
        for s in range(BATCH // GROUP):
            at = start + s * GROUP
            block = jnp.concatenate(
                [landed[pl.ds(at, GROUP), 16 * q : 16 * q + 16, :].reshape(256, 128) for q in range(QUADS)], axis=1
            )
            flat = dot(unpack, block).astype(BF16)
            for q in range(QUADS):
                for b in range(4):
                    x_rows[64 * s : 64 * s + 64, (4 * q + b) * 128 : (4 * q + b) * 128 + 128] = flat[
                        64 * b : 64 * b + 64, 128 * q : 128 * q + 128
                    ]
        rows = x_rows[:, 0:D]
        gate_value = dot_nt(rows, gu_v[0])
        up_value = dot_nt(rows, gu_v[1])
        hidden = ((up_value + 1.0) * gate_value * jax.nn.sigmoid(1.702 * gate_value)).astype(BF16)
        o_rows[:, 0:D] = dot(hidden, down_v[...]).astype(BF16)
        for s in range(BATCH // GROUP):
            at = start + s * GROUP
            block = jnp.concatenate(
                [
                    jnp.concatenate(
                        [
                            o_rows[64 * s : 64 * s + 64, (4 * q + b) * 128 : (4 * q + b) * 128 + 128]
                            for b in range(4)
                        ],
                        axis=0,
                    )
                    for q in range(QUADS)
                ],
                axis=1,
            )
            flat = dot(repack, block).astype(BF16)
            for q in range(QUADS):
                back[pl.ds(at, GROUP), 16 * q : 16 * q + 16, :] = flat[:, 128 * q : 128 * q + 128].reshape(
                    GROUP, 16, 128
                )
        lax.fori_loop(jnp.maximum(start, 1), start + BATCH, give, 0)
        return carry

    lax.fori_loop(0, PEERS // BATCH, batch, 0)
    own_back = pltpu.make_async_copy(back.at[0], home.at[0], home_recv.at[0])
    own_back.start()

    for copy in later:
        copy.wait()
    def fold(g):
        return (((iota((512, 256), 0) & 63) + 64 * g) == iota((512, 256), 1)).astype(BF16)

    own_head = (iota((64, 512), 1) >> 6) == (iota((64, 512), 0) & 7)
    for g in range(4):
        part = jnp.concatenate([queries[r, :, 512 * g : 512 * g + 512].astype(F32) for r in range(4)], axis=0) * 0.125
        part = jnp.broadcast_to(part[:, None, :], (8, 8, 512)).reshape(64, 512)
        part = jnp.where(own_head, part, 0.0).astype(BF16)
        folded = dot(part, fold(g)).astype(BF16)
        spread[:, 16 * g : 16 * g + 16, :] = folded.reshape(4, 16, 256)
    take = iota((16, 16), 1)
    take_at = iota((16, 16), 0)
    fresh_rows = jnp.concatenate([fresh[r, i].astype(F32) for r in range(4) for i in range(2)], axis=0).astype(BF16)
    fresh_keys = dot(((2 * take_at == take) & (take_at < 8)).astype(BF16), fresh_rows).astype(BF16)
    fresh_values = dot(((2 * take_at + 1 == take) & (take_at < 8)).astype(BF16), fresh_rows).astype(BF16)
    sink_row = iota((64, 32), 0)
    sink_at = (sink_row >> 4) * 8 + (sink_row & 7) == iota((64, 32), 1)
    sink = jnp.sum(jnp.where(sink_at, sinks[...], 0.0), axis=1, keepdims=True)
    pool_copy.wait()

    def request(r, carry):
        query = spread[r]
        limit = length[r]
        fresh_col = iota((64, 16), 1)
        fresh_row = iota((64, 16), 0)
        fresh_ok = ((fresh_col >> 1) == r) & ((fresh_col & 1) <= ((fresh_row >> 3) & 1))
        fresh_scores = jnp.where(fresh_ok, dot_nt(query, fresh_keys), NEG)
        top = jnp.maximum(jnp.max(fresh_scores, axis=1, keepdims=True), sink)
        best = jnp.full((64, 256), NEG, F32)
        for b in range(8):
            keys = jnp.concatenate([pool_v[table[r, 4 * b + i], 0] for i in range(4)], axis=0)
            block = dot_nt(query, keys)
            block = jnp.where(iota((64, 256), 1) + 256 * b < limit, block, NEG)
            scores[:, 256 * b : 256 * b + 256] = block
            best = jnp.maximum(best, block)
        top = jnp.maximum(top, jnp.max(best, axis=1, keepdims=True))
        fresh_exp = jnp.where(fresh_ok, jnp.exp(fresh_scores - top), 0.0)
        result = dot(fresh_exp.astype(BF16), fresh_values)
        summed = jnp.zeros((64, 256), F32)
        for b in range(8):
            ok = iota((64, 256), 1) + 256 * b < limit
            block = jnp.where(ok, jnp.exp(scores[:, 256 * b : 256 * b + 256] - top), 0.0)
            summed = summed + block
            values = jnp.concatenate([pool_v[table[r, 4 * b + i], 1] for i in range(4)], axis=0)
            result = result + dot(block.astype(BF16), values)
        denominator = (
            jnp.exp(sink - top)
            + jnp.sum(fresh_exp, axis=1, keepdims=True)
            + jnp.sum(summed, axis=1, keepdims=True)
        )
        outs[r] = (result / denominator).astype(BF16)
        return carry

    lax.fori_loop(0, 4, request, 0)
    for g in range(4):
        part = outs[:, 16 * g : 16 * g + 16, :].reshape(64, 256)
        part = jnp.where(own_head, dot_nt(part, fold(g)), 0.0)
        part = jnp.sum(part.reshape(8, 8, 512), axis=1)
        for r in range(4):
            attended[r, :, 512 * g : 512 * g + 512] = part[2 * r : 2 * r + 2].astype(BF16)

    swap = pltpu.make_async_remote_copy(
        src_ref=given, dst_ref=partial, send_sem=pair_send.at[1], recv_sem=pair_recv.at[1],
        device_id=sibling, device_id_type=MESH,
    )
    for k in range(PEERS // GROUP):
        homeward(pl.ds(GROUP * k, GROUP), k).wait_recv()
        block = jnp.concatenate(
            [home[GROUP * k : GROUP * (k + 1), 16 * q : 16 * q + 16, :].reshape(256, 128) for q in range(QUADS)],
            axis=1,
        )
        for half in range(2):
            both = dot(weights[128 * half : 128 * half + 128, 256 * k : 256 * k + 256], block)
            here = both[0:64] + both[64:128]
            if k:
                here = here + total[half]
            total[half] = here
            if half == 0 and k == PEERS // GROUP - 1:
                given[...] = here.astype(BF16)
                swap.start()

    outward(pl.ds(1, PEERS - 1), 0).wait_send()
    homeward(pl.ds(1, PEERS - 1), 0).wait_send()
    pair.wait_send()
    swap.wait()
    for n in range(23):
        q, b = n // 4, n % 4
        width = min(128, D - 128 * n)
        at = slice(128 * n, 128 * n + width)
        part = (slice(16 * b, 16 * b + 16), slice(128 * q, 128 * q + width))
        mixed[:, at] = (tokens[:, at].astype(F32) + total[(1, *part)] + partial[part].astype(F32)).astype(BF16)


def finish(mixed_in, attended_in, mixed, attended, sem):
    copies = [
        pltpu.make_async_copy(mixed_in, mixed, sem.at[0]),
        pltpu.make_async_copy(attended_in, attended, sem.at[1]),
    ]
    for copy in copies:
        copy.start()
    for copy in copies:
        copy.wait()


def local(
    tokens, norm_gain, expert_ids, gate_weights, expert_gate_up, expert_down,
    queries, new_cache, cache_pool, page_table, cache_length, sink_logits,
):
    hbm = pl.BlockSpec(memory_space=pl.ANY)
    vmem = pl.BlockSpec(memory_space=pltpu.VMEM)
    dma = pltpu.SemaphoreType.DMA
    packed = pltpu.VMEM((PEERS, ROWS, 128), BF16)
    shapes = (
        jax.ShapeDtypeStruct((16, D), BF16),
        jax.ShapeDtypeStruct((4, 2, 2048), BF16),
    )
    mixed, attended = pl.pallas_call(
        kernel,
        out_shape=(pltpu.VMEM((16, D), BF16), pltpu.VMEM((4, 2, 2048), BF16)),
        in_specs=[hbm] * 12,
        out_specs=(vmem, vmem),
        scratch_shapes=[
            pltpu.VMEM((16, D), BF16),
            pltpu.VMEM((D,), F32),
            pltpu.VMEM((4, 16), jnp.int32),
            pltpu.VMEM((4, 16), F32),
            pltpu.VMEM((4, 2, 2048), BF16),
            pltpu.VMEM((4, 2, 2, 256), BF16),
            pltpu.VMEM((1, 32), F32),
            pltpu.SMEM((4, 32), jnp.int32),
            pltpu.SMEM((4,), jnp.int32),
            pltpu.VMEM((16, WIDE), BF16),
            pltpu.VMEM((16, WIDE), BF16),
            packed,
            packed,
            packed,
            packed,
            pltpu.VMEM((4 * BATCH, WIDE), BF16),
            pltpu.VMEM((4 * BATCH, WIDE), BF16),
            pltpu.VMEM((256, 1024), BF16),
            pltpu.VMEM((2, 64, 768), F32),
            pltpu.VMEM((64, 768), BF16),
            pltpu.VMEM((64, 768), BF16),
            pltpu.VMEM((2, H, D), BF16),
            pltpu.VMEM((H, D), BF16),
            pltpu.VMEM((128, 2, 64, 256), BF16),
            pltpu.VMEM((4, 64, 256), BF16),
            pltpu.VMEM((64, 2048), F32),
            pltpu.VMEM((4, 64, 256), BF16),
            dma((12,)),
            dma((2,)),
            dma((2,)),
            dma((2,)),
            dma((PEERS // GROUP,)),
            dma((PEERS // GROUP,)),
        ],
        compiler_params=pltpu.CompilerParams(
            collective_id=0, has_side_effects=True, vmem_limit_bytes=56 * 2**20
        ),
        name="decode",
    )(
        tokens, norm_gain, expert_ids.T, gate_weights.T, expert_gate_up.transpose(0, 1, 3, 2), expert_down,
        queries, new_cache, cache_pool, page_table, cache_length,
        sink_logits.reshape(1, 32),
    )
    return pl.pallas_call(
        finish,
        out_shape=shapes,
        in_specs=[vmem] * 2,
        out_specs=(hbm, hbm),
        scratch_shapes=[dma((2,))],
        compiler_params=pltpu.CompilerParams(vmem_limit_bytes=4 * 2**20),
        name="finish",
    )(mixed, attended)


def solution(mesh):
    rows = P(("dp", "ep"))
    placed = (rows, P(), rows, rows, rows, rows, rows, rows, rows, rows, rows, P())
    return jax.shard_map(
        local, mesh=mesh, in_specs=placed, out_specs=(rows, rows), check_vma=False
    )
```
